512 devices in a mesh: pipe: 4 (over y), seq: 16 (over z), tensor: 8 (over x, core).
Axes of the slice: x: 4, y: 4, z: 16, core: 2. Of those that a mesh axis runs over, the one named last changes fastest.
Arguments:
- layer_input: bfloat16 [4, 2048, 8192], P('pipe', 'seq', 'tensor'), may hold values from -320 to 320
- conv_out: bfloat16 [4, 2048, 8192], P('pipe', 'seq', 'tensor'), may hold values from -8 to 8
- act_grad: bfloat16 [4, 2048, 8192], P('pipe', 'seq', 'tensor'), may hold values from -6 to 6
- conv_kernel: bfloat16 [4, 4, 8192], P('pipe', None, 'tensor'), may hold values from -3 to 3
- in_proj: bfloat16 [4, 8192, 8192], P('pipe', 'seq', 'tensor'), may hold values from -0.0625 to 0.0625
- sketch_matrix: bfloat16 [4, 8192, 512], P('pipe', 'tensor'), may hold values from -0.0625 to 0.0625
Outputs:
- passed_grad: bfloat16 [4, 2048, 8192], P('pipe', 'tensor', 'seq')
- basis: bfloat16 [4, 8192, 512], P('pipe', 'tensor')
The draws below stay inside these ranges and needn't reach their ends.
All inputs are finite; a program needn't handle non-finite values.
Results may differ from the reference program's by a relative error of at most 0.017.
Values may be sent and summed in bfloat16 or wider, within the bound.
No kernel may reach another device: no remote copies, remote signals or barrier semaphores. Data moves between devices by JAX's collectives and lax.ppermute only.
A program may use at most 64 MiB of HBM per device.

```python
import math
import jax
import jax.numpy as jnp
from jax import lax

D = 8192
E = 8192
R = 512
KW = 4
TOKENS = 2048
SECTIONS = 4
N_TENSOR = 8


def draw_layer_input(key, part):
    key_values = jax.random.fold_in(key, 11)
    key_columns = jax.random.fold_in(key, 12)
    column = jnp.arange(D, dtype=jnp.float32) / D
    jitter = jax.random.uniform(key_columns, (SECTIONS, 1, D), jnp.float32, 0.7, 1.4)
    scales = jnp.power(10.0, 1.5 * column)[None, None, :] * jitter
    values = jax.random.truncated_normal(key_values, -4.0, 4.0, (SECTIONS, TOKENS, D), jnp.float32)
    return (values * scales).astype(jnp.bfloat16)


def shard_levels(rng, extent, cuts, low, largest):
    loudness, own = 1.0, jax.random.fold_in(rng, 6)
    for dim, parts in cuts:
        draws = jnp.exp(jax.random.uniform(jax.random.fold_in(own, dim), (parts,), jnp.float32, low / len(cuts), largest / len(cuts)))
        loudness = loudness * jnp.repeat(draws, extent[dim] // parts).reshape([-1 if axis == dim else 1 for axis in range(len(extent))])
    return loudness


def gaussian(rng, dims, spread, most, pieces=(), held_as=jnp.bfloat16):
    entries = spread * jax.random.normal(rng, dims, jnp.float32)
    if pieces:
        entries = entries * shard_levels(rng, dims, pieces, -0.22, 0.18)
    return jnp.clip(entries, -most, most).astype(held_as)


def setup_inputs(seed: int = 0) -> dict:
    key_list = jax.random.split(jax.random.key(seed), 7)
    layer_input = draw_layer_input(jax.random.fold_in(key_list[6], 71), 0)
    conv_out = gaussian(key_list[1], (SECTIONS, TOKENS, E), 1.5, 8.0, ((0, 4), (1, 16), (2, 8)))
    act_grad = gaussian(key_list[2], (SECTIONS, TOKENS, E), 1.0, 6.0, ((0, 4), (1, 16), (2, 8)))
    conv_kernel = gaussian(key_list[3], (SECTIONS, KW, E), 0.5, 3.0, ((0, 4), (2, 8)))
    in_proj = gaussian(key_list[4], (SECTIONS, D, E), E ** -0.5, 0.0625, ((0, 4), (1, 16), (2, 8)))
    sketch_matrix = gaussian(key_list[5], (SECTIONS, E, R), E ** -0.5, 0.0625, ((0, 4), (1, 8)))
    return {"layer_input": layer_input, "conv_out": conv_out, "act_grad": act_grad, "conv_kernel": conv_kernel, "in_proj": in_proj, "sketch_matrix": sketch_matrix}


def one_section(items):
    layer_input, conv_out, act_grad, conv_kernel, in_proj, sketch_matrix = items
    pval = conv_out.astype(jnp.float32)
    sig = jax.nn.sigmoid(pval)
    pre_grad = act_grad.astype(jnp.float32) * sig * (1.0 + pval * (1.0 - sig))
    extended = jnp.concatenate([pre_grad, jnp.zeros((KW - 1, E), jnp.float32)], axis=0)
    total = jnp.zeros((TOKENS, E), jnp.float32)
    for tap in range(KW):
        total = total + conv_kernel[tap].astype(jnp.float32) * extended[tap:tap + TOKENS]
    in_grad = total.astype(jnp.bfloat16)
    width = E // N_TENSOR
    grad_groups = in_grad.reshape(TOKENS, N_TENSOR, width).transpose(1, 0, 2)
    weight_groups = in_proj.reshape(D, N_TENSOR, width).transpose(1, 0, 2)

    def add_group(carry, pair):
        term = jnp.dot(pair[0].astype(jnp.float32), pair[1].T.astype(jnp.float32), preferred_element_type=jnp.float32).astype(jnp.bfloat16)
        term = lax.optimization_barrier(term)
        return (carry + term.astype(jnp.float32), None)
    summed, unused = lax.scan(add_group, jnp.zeros((TOKENS, D), jnp.float32), (grad_groups, weight_groups))
    input_grad = summed.astype(jnp.bfloat16)
    sketch_rows = jnp.dot(in_grad.astype(jnp.float32), sketch_matrix.astype(jnp.float32), preferred_element_type=jnp.float32).astype(jnp.bfloat16)
    sketch = jnp.dot(layer_input.T.astype(jnp.float32), sketch_rows.astype(jnp.float32), preferred_element_type=jnp.float32)
    gram = jnp.dot(sketch.T, sketch, precision=lax.Precision.HIGHEST)
    low = jnp.linalg.cholesky(gram)
    ortho_t = lax.linalg.triangular_solve(low, sketch.T, left_side=True, lower=True)
    basis = (ortho_t.T * math.sqrt(D)).astype(jnp.bfloat16)
    return (input_grad, basis)

def reference(layer_input, conv_out, act_grad, conv_kernel, in_proj, sketch_matrix):
    input_grads, basis = lax.map(one_section, (layer_input, conv_out, act_grad, conv_kernel, in_proj, sketch_matrix))
    passed_grad = jnp.roll(input_grads, -1, axis=0)
    return (passed_grad, basis)
```

```python
import functools
import math

import jax
import jax.numpy as jnp
from jax import lax
from jax.experimental import pallas as pl
from jax.experimental.pallas import tpu as pltpu
from jax.sharding import PartitionSpec as P

D = 8192
F = jnp.float32
B = jnp.bfloat16
HI = lax.Precision.HIGHEST
VMEM = pl.BlockSpec(memory_space=pltpu.VMEM)
LIMIT = 32 * 1024 * 1024
WIDE = 58 * 1024 * 1024


def row_of(x, i):
    return jnp.broadcast_to(x[i:i+1, :], x.shape)
def lane_of(x, l):
    return jnp.broadcast_to(x[:, l:l+1], (x.shape[0], 128))

def leaf(work):
    sub = lax.broadcasted_iota(jnp.int32, (8, 128), 0)
    for p in range(16):
        pa = work[8*p:8*p+8, 0:128]
        pi = work[8*p:8*p+8, 128:256]
        cols = [lane_of(pa, 8*p+j) for j in range(8)]
        e = {}
        for j in range(8):
            for i in range(j, 8):
                e[i, j] = row_of(cols[j], i)
        x = {}; l = {}
        for j in range(8):
            r = lax.rsqrt(e[j, j])
            x[j, j] = r
            for i in range(j+1, 8):
                l[i, j] = e[i, j] * r
            for i in range(j+1, 8):
                for k in range(j+1, i+1):
                    e[i, k] = e[i, k] - l[i, j] * l[k, j]
        for j in range(8):
            for i in range(j+1, 8):
                acc = l[i, j] * x[j, j]
                for k in range(j+1, i):
                    acc = acc + l[i, k] * x[k, j]
                x[i, j] = -x[i, i] * acc
        ra = [row_of(pa, j) for j in range(8)]
        ri = [row_of(pi, j) for j in range(8)]
        ta = []; ti = []
        for i in range(8):
            a = x[i, 0]*ra[0]; b = x[i, 0]*ri[0]
            for j in range(1, i+1):
                a = a + x[i, j]*ra[j]; b = b + x[i, j]*ri[j]
            ta.append(a); ti.append(b)
        if p < 15:
            wa = []; wi = []
            for i in range(8):
                a = x[i, i]*ta[i]; b = x[i, i]*ti[i]
                for j in range(i+1, 8):
                    a = a + x[j, i]*ta[j]; b = b + x[j, i]*ti[j]
                wa.append(a); wi.append(b)
            for q in range(p+1, 16):
                qa = work[8*q:8*q+8, 0:128]
                qi = work[8*q:8*q+8, 128:256]
                cs = [lane_of(qa, 8*p+j) for j in range(8)]
                da = cs[0]*wa[0]; di = cs[0]*wi[0]
                for j in range(1, 8):
                    da = da + cs[j]*wa[j]; di = di + cs[j]*wi[j]
                work[8*q:8*q+8, 0:128] = qa - da
                work[8*q:8*q+8, 128:256] = qi - di
        ui = ti[0]
        for j in range(1, 8):
            ui = jnp.where(sub == j, ti[j], ui)
        work[8*p:8*p+8, 128:256] = ui

def dot(a, b, ca, cb, prec=HI):
    return lax.dot_general(a, b, (((ca,), (cb,)), ((), ())), precision=prec, preferred_element_type=F)

def split(x):
    hi = x.astype(B)
    return hi, (x - hi.astype(F)).astype(B)

def chol_kernel(scale, gram_ref, sketch_ref, out_ref, m, work):
    n = 4
    blk = 0
    for r in range(n):
        for c in range(r, n):
            m[r*128:(r+1)*128, c*128:(c+1)*128] = gram_ref[blk*128:(blk+1)*128, :]
            blk += 1
    eye = (lax.broadcasted_iota(jnp.int32, (128, 128), 0) == lax.broadcasted_iota(jnp.int32, (128, 128), 1)).astype(F)
    def stage(k, carry):
        base = pl.multiple_of(k*128, 128)
        work[:, 0:128] = m[pl.ds(base, 128), pl.ds(base, 128)]
        work[:, 128:256] = eye
        leaf(work)
        inv = work[:, 128:256]
        m[pl.ds(base, 128), pl.ds(base, 128)] = eye
        row = dot(inv, m[pl.ds(base, 128), :], 1, 0)
        m[pl.ds(base, 128), :] = row
        def update(j, carry):
            jb = pl.multiple_of(j*128, 128)
            ukj = m[pl.ds(base, 128), pl.ds(jb, 128)]
            m[pl.ds(jb, 128), pl.ds(base, 128)] = jnp.zeros((128, 128), F)
            m[pl.ds(jb, 128), :] -= dot(ukj, m[pl.ds(base, 128), :], 0, 0)
            return carry
        lax.fori_loop(k+1, n, update, 0)
        return carry
    lax.fori_loop(0, n, stage, 0)
    for r in range(n):
        for c in range(r+1, n):
            m[r*128:(r+1)*128, c*128:(c+1)*128] = jnp.zeros((128, 128), F)
    th, tl = split(m[...] * scale)
    def body(i, carry):
        b = pl.multiple_of(i*256, 256)
        sh, sl = split(sketch_ref[pl.ds(b, 256), :])
        d = dot(sh, th, 1, 1, None) + (dot(sh, tl, 1, 1, None) + dot(sl, th, 1, 1, None))
        out_ref[pl.ds(b, 256), :] = d.astype(B)
        return carry
    lax.fori_loop(0, sketch_ref.shape[0]//256, body, 0)

def finish(gram_packed, sketch, scale, **kw):
    return pl.pallas_call(
        functools.partial(chol_kernel, scale),
        out_shape=jax.ShapeDtypeStruct(sketch.shape, B),
        in_specs=[pl.BlockSpec(memory_space=pltpu.VMEM)]*2,
        out_specs=pl.BlockSpec(memory_space=pltpu.VMEM),
        scratch_shapes=[pltpu.VMEM((512, 512), F), pltpu.VMEM((128, 256), F)],
        compiler_params=pltpu.CompilerParams(vmem_limit_bytes=LIMIT), **kw,
    )(gram_packed, sketch)


def front_kernel(conv_ref, act_ref, next_ref, taps_ref, acts_ref, test_ref, both_ref, rows_ref, held):
    rows = conv_ref.shape[0]

    def pre(p, g):
        sig = jax.nn.sigmoid(p)
        return g * sig * (1.0 + p * (1.0 - sig))

    held[0:rows, :] = pre(conv_ref[...].astype(F), act_ref[...].astype(F))
    after = next_ref[...].astype(F)
    held[rows : rows + 8, :] = pre(after[0:8, :], after[8:16, :])
    taps = taps_ref[...].astype(F)
    total = taps[0:1, :] * held[0:rows, :]
    for tap in range(1, taps.shape[0]):
        total = total + taps[tap : tap + 1, :] * held[tap : tap + rows, :]
    grad = total.astype(B)
    both_ref[0:rows, :] = acts_ref[...]
    both_ref[rows : 2 * rows, :] = grad
    rows_ref[...] = jnp.dot(grad, test_ref[...], preferred_element_type=F)


def front(conv, act, after, taps, acts, test):
    rows, width = conv.shape
    return pl.pallas_call(
        front_kernel,
        out_shape=(
            jax.ShapeDtypeStruct((2 * rows, width), B),
            jax.ShapeDtypeStruct((rows, test.shape[1]), F),
        ),
        scratch_shapes=[pltpu.VMEM((rows + 8, width), F)],
        compiler_params=pltpu.CompilerParams(vmem_limit_bytes=WIDE),
    )(conv, act, after, taps, acts, test)


def grad_kernel(grad_ref, weight_ref, out_ref):
    grad = grad_ref[...].reshape(-1, grad_ref.shape[-1])
    out_ref[...] = lax.dot_general(
        grad, weight_ref[...], (((1,), (1,)), ((), ())), preferred_element_type=F
    ).astype(B)


def grad_terms(gathered, weights):
    shards, twice, width = gathered.shape
    rows = twice // 2
    each = 4
    return pl.pallas_call(
        grad_kernel,
        grid=(shards // each,),
        out_shape=jax.ShapeDtypeStruct((shards * rows, weights.shape[0]), B),
        in_specs=[
            pl.BlockSpec((each, rows, width), lambda i: (i, 1, 0)),
            pl.BlockSpec(weights.shape, lambda i: (0, 0)),
        ],
        out_specs=pl.BlockSpec((each * rows, weights.shape[0]), lambda i: (i, 0)),
        compiler_params=pltpu.CompilerParams(vmem_limit_bytes=WIDE),
    )(gathered, weights)


def sketch_kernel(acts_ref, rows_ref, sketch_ref, gram_ref):
    groups, shards, share, rank = rows_ref.shape
    cols = acts_ref.shape[-1]
    part = jnp.zeros((cols, rank), F)
    for g in range(groups):
        acts = acts_ref[:, g * share : (g + 1) * share, :].reshape(shards * share, cols)
        rows = rows_ref[g].reshape(shards * share, rank)
        part += lax.dot_general(acts, rows, (((0,), (0,)), ((), ())), preferred_element_type=F)
    sketch_ref[...] = part

    @pl.when(pl.program_id(0) == 0)
    def _():
        gram_ref[...] = jnp.zeros(gram_ref.shape, F)

    at = 0
    for r in range(part.shape[1] // 128):
        terms = dot(part[:, r * 128 : (r + 1) * 128], part[:, r * 128 :], 0, 0)
        for c in range(terms.shape[1] // 128):
            gram_ref[at : at + 128, :] += terms[:, c * 128 : (c + 1) * 128]
            at += 128


def sketch_and_gram(gathered, rows):
    shards, twice, width = gathered.shape
    cols = 256
    rank = rows.shape[-1]
    blocks = rank // 128
    packed = blocks * (blocks + 1) // 2 * 128
    return pl.pallas_call(
        sketch_kernel,
        grid=(width // cols,),
        out_shape=(
            jax.ShapeDtypeStruct((width, rank), F),
            jax.ShapeDtypeStruct((packed, 128), F),
        ),
        in_specs=[
            pl.BlockSpec((shards, twice // 2, cols), lambda i: (0, 0, i)),
            pl.BlockSpec(rows.shape, lambda i: (0, 0, 0, 0)),
        ],
        out_specs=(
            pl.BlockSpec((cols, rank), lambda i: (i, 0)),
            pl.BlockSpec((packed, 128), lambda i: (0, 0)),
        ),
        compiler_params=pltpu.CompilerParams(vmem_limit_bytes=WIDE),
    )(gathered, rows)


def gathered_rows(terms):
    groups = lax.axis_size("tensor")
    rank = terms.shape[1]
    terms = lax.all_to_all(terms.reshape(groups, -1, rank), "tensor", 0, 0, tiled=True)
    rows = jnp.sum(terms, axis=0).astype(B)
    rows = lax.all_gather(rows, "seq", axis=0)
    return lax.all_to_all(
        jnp.broadcast_to(rows[None], (groups,) + rows.shape), "tensor", 0, 0, tiled=True
    )


def local(layer_input, conv_out, act_grad, conv_kernel, in_proj, sketch_matrix):
    conv, act = conv_out[0], act_grad[0]
    shards = lax.axis_size("seq")
    after = lax.ppermute(
        jnp.concatenate([conv[:8], act[:8]], axis=0),
        "seq",
        [(i + 1, i) for i in range(shards - 1)],
    )
    both, row_terms = front(conv, act, after, conv_kernel[0], layer_input[0], sketch_matrix[0])
    gathered = lax.all_gather(both, "seq", axis=0)
    rows = gathered_rows(row_terms)
    gathered, rows = lax.optimization_barrier((gathered, rows))
    terms = grad_terms(gathered, in_proj[0])
    input_grad = lax.psum_scatter(terms, "tensor", scatter_dimension=0, tiled=True)
    count = lax.axis_size("pipe")
    passed = lax.ppermute(input_grad, "pipe", [(i, (i - 1) % count) for i in range(count)])
    sketch, gram = sketch_and_gram(gathered, rows)
    groups = lax.axis_size("tensor")
    gram = lax.all_to_all(gram.reshape(groups, -1, 128), "tensor", 0, 0, tiled=True)
    gram = lax.all_gather(jnp.sum(gram, axis=0), "tensor", axis=0, tiled=True)
    basis = finish(gram, sketch, math.sqrt(D))
    return (passed[None], basis[None])


def solution(mesh):
    placed = (
        P("pipe", "seq", "tensor"),
        P("pipe", "seq", "tensor"),
        P("pipe", "seq", "tensor"),
        P("pipe", None, "tensor"),
        P("pipe", "seq", "tensor"),
        P("pipe", "tensor", None),
    )
    return jax.shard_map(
        local,
        mesh=mesh,
        in_specs=placed,
        out_specs=(P("pipe", "tensor", "seq"), P("pipe", "tensor", None)),
        check_vma=False,
    )
```

```python
import functools
import math

import jax
import jax.numpy as jnp
from jax import lax
from jax.experimental import pallas as pl
from jax.experimental.pallas import tpu as pltpu
from jax.sharding import PartitionSpec as P

D = 8192
F = jnp.float32
B = jnp.bfloat16
HI = lax.Precision.HIGHEST
VMEM = pl.BlockSpec(memory_space=pltpu.VMEM)
ANY = pl.BlockSpec(memory_space=pl.ANY)
LIMIT = 32 * 1024 * 1024
WIDE = 58 * 1024 * 1024
EDGE = 16


def dot(a, b, ca, cb, prec=HI):
    return lax.dot_general(
        a, b, (((ca,), (cb,)), ((), ())), precision=prec, preferred_element_type=F
    )


def split(x):
    hi = x.astype(B)
    return hi, (x - hi.astype(F)).astype(B)


def total_of(values):
    values = list(values)
    while len(values) > 1:
        values = [
            values[i] + values[i + 1] if i + 1 < len(values) else values[i]
            for i in range(0, len(values), 2)
        ]
    return values[0]


def pre_grad(p, g):
    sig = jax.nn.sigmoid(p)
    return g * sig * (1.0 + p * (1.0 - sig))


def convolved(held, taps, rows):
    total = taps[0:1, :] * held[0:rows, :]
    for tap in range(1, taps.shape[0]):
        total = total + taps[tap : tap + 1, :] * held[tap : tap + rows, :]
    return total.astype(B)


def front_kernel(conv_ref, act_ref, taps_ref, acts_ref, both_ref, held):
    rows = conv_ref.shape[0]
    held[0:rows, :] = pre_grad(conv_ref[...].astype(F), act_ref[...].astype(F))
    held[rows : rows + 8, :] = jnp.zeros((8, held.shape[1]), F)
    both_ref[0:rows, :] = acts_ref[...]
    both_ref[rows : 2 * rows, :] = convolved(held, taps_ref[...].astype(F), rows)


def front(conv, act, taps, acts):
    rows, width = conv.shape
    return pl.pallas_call(
        front_kernel,
        out_shape=jax.ShapeDtypeStruct((2 * rows, width), B),
        scratch_shapes=[pltpu.VMEM((rows + 8, width), F)],
        compiler_params=pltpu.CompilerParams(vmem_limit_bytes=WIDE),
    )(conv, act, taps, acts)


def edge_kernel(conv_ref, act_ref, next_ref, taps_ref, grad_ref, test_ref, rows_ref, edge_ref, held):
    held[0:EDGE, :] = pre_grad(conv_ref[...].astype(F), act_ref[...].astype(F))
    after = next_ref[...].astype(F)
    held[EDGE : EDGE + 8, :] = pre_grad(after[0:8, :], after[8:16, :])
    edge = convolved(held, taps_ref[...].astype(F), EDGE)
    half = edge.shape[1] // 2
    edge_ref[0:EDGE, :] = edge[:, 0:half]
    edge_ref[EDGE : 2 * EDGE, :] = edge[:, half:]
    rows = grad_ref.shape[0]
    grad = jnp.concatenate([grad_ref[0 : rows - EDGE, :], edge], axis=0)
    rows_ref[...] = jnp.dot(grad, test_ref[...], preferred_element_type=F)


def edge_and_rows(conv, act, after, taps, both, test):
    rows, width = conv.shape
    rank = test.shape[1]
    last = rows // EDGE - 1

    def whole(*shape):
        return pl.BlockSpec(shape, lambda i: (0, 0))

    return pl.pallas_call(
        edge_kernel,
        grid=(1,),
        out_shape=(
            jax.ShapeDtypeStruct((rows, rank), F),
            jax.ShapeDtypeStruct((2 * EDGE, width // 2), B),
        ),
        in_specs=[
            pl.BlockSpec((EDGE, width), lambda i: (last, 0)),
            pl.BlockSpec((EDGE, width), lambda i: (last, 0)),
            whole(*after.shape),
            whole(*taps.shape),
            pl.BlockSpec((rows, width), lambda i: (1, 0)),
            whole(*test.shape),
        ],
        out_specs=(whole(rows, rank), whole(2 * EDGE, width // 2)),
        scratch_shapes=[pltpu.VMEM((EDGE + 8, width), F)],
        compiler_params=pltpu.CompilerParams(vmem_limit_bytes=WIDE),
    )(conv, act, after, taps, both, test)


CHUNKS = 4


def middle_kernel(
    both_ref, rows_ref, edge_ref, weight_ref, sketch_ref, gram_ref, terms_ref,
    acts, grads, terms, right_all, weights, in_sems, out_sems,
):
    shards, twice, width = both_ref.shape
    tokens = twice // 2
    groups, _, share, rank = rows_ref.shape
    cols = width // CHUNKS
    each = shards // CHUNKS

    def acts_copy(i):
        return pltpu.make_async_copy(
            both_ref.at[:, 0:tokens, i * cols : (i + 1) * cols], acts.at[i], in_sems.at[i]
        )

    def grads_copy(i):
        return pltpu.make_async_copy(
            both_ref.at[i * each : (i + 1) * each, tokens:twice, :], grads.at[i], in_sems.at[CHUNKS + i]
        )

    def terms_copy(i):
        return pltpu.make_async_copy(
            terms.at[i], terms_ref.at[i * each * tokens : (i + 1) * each * tokens, :], out_sems.at[i]
        )

    rows_copy = pltpu.make_async_copy(rows_ref, right_all, in_sems.at[2 * CHUNKS])
    weight_copy = pltpu.make_async_copy(weight_ref, weights, in_sems.at[2 * CHUNKS + 1])
    acts_copy(0).start()
    rows_copy.start()
    for i in range(1, CHUNKS):
        acts_copy(i).start()
    weight_copy.start()
    for i in range(CHUNKS):
        grads_copy(i).start()
    rows_copy.wait()
    for i in range(CHUNKS):
        acts_copy(i).wait()
        part = jnp.zeros((cols, rank), F)
        for g in range(groups):
            left = acts[i, :, g * share : (g + 1) * share, :].reshape(shards * share, cols)
            right = right_all[g].reshape(shards * share, rank)
            part += dot(left, right, 0, 0, None)
        sketch_ref[i * cols : (i + 1) * cols, :] = part
        at = 0
        for r in range(rank // 128):
            block = dot(part[:, r * 128 : (r + 1) * 128], part[:, r * 128 :], 0, 0)
            for c in range(block.shape[1] // 128):
                piece = block[:, c * 128 : (c + 1) * 128]
                if i == 0:
                    gram_ref[at : at + 128, :] = piece
                else:
                    gram_ref[at : at + 128, :] += piece
                at += 128
    half = width // 2
    weight_copy.wait()
    for i in range(CHUNKS):
        grads_copy(i).wait()
        for z in range(each):
            edge = edge_ref[i * each + z]
            grads[i, z, tokens - EDGE : tokens, 0:half] = edge[0:EDGE, :]
            grads[i, z, tokens - EDGE : tokens, half:] = edge[EDGE : 2 * EDGE, :]
        left = grads[i].reshape(each * tokens, width)
        terms[i] = dot(left, weights[...], 1, 1, None).astype(B)
        terms_copy(i).start()
    for i in range(CHUNKS):
        terms_copy(i).wait()


def middle(gathered, rows, edges, weights):
    shards, twice, width = gathered.shape
    tokens = twice // 2
    rank = rows.shape[-1]
    blocks = rank // 128
    packed = blocks * (blocks + 1) // 2 * 128
    outs = weights.shape[0]
    each = shards // CHUNKS
    return pl.pallas_call(
        middle_kernel,
        out_shape=(
            jax.ShapeDtypeStruct((width, rank), F),
            jax.ShapeDtypeStruct((packed, 128), F),
            jax.ShapeDtypeStruct((shards * tokens, outs), B),
        ),
        in_specs=[ANY, ANY, VMEM, ANY],
        out_specs=(VMEM, VMEM, ANY),
        scratch_shapes=[
            pltpu.VMEM((CHUNKS, shards, tokens, width // CHUNKS), B),
            pltpu.VMEM((CHUNKS, each, tokens, width), B),
            pltpu.VMEM((CHUNKS, each * tokens, outs), B),
            pltpu.VMEM(rows.shape, B),
            pltpu.VMEM(weights.shape, B),
            pltpu.SemaphoreType.DMA((2 * CHUNKS + 2,)),
            pltpu.SemaphoreType.DMA((CHUNKS,)),
        ],
        compiler_params=pltpu.CompilerParams(vmem_limit_bytes=WIDE),
    )(gathered, rows, edges, weights)


def lane_of(x, l):
    return jnp.broadcast_to(x[:, l : l + 1], (8, 128))


def row_of(ref, r, c):
    return jnp.broadcast_to(ref[r : r + 1, c : c + 128], (8, 128))


def leaf(work, staged):
    sub = lax.broadcasted_iota(jnp.int32, (8, 128), 0)
    for p in range(16):
        top = 8 * p
        panel = work[top : top + 8, 0:128]
        left = [row_of(work, top + j, 0) for j in range(8)]
        right = [row_of(work, top + j, 128) for j in range(8)]
        e = {}
        for j in range(8):
            staged[8 * j : 8 * j + 8, :] = lane_of(panel, top + j)
            for i in range(j, 8):
                e[i, j] = row_of(staged, 8 * j + i, 0)
        inv = {}
        acc = {}
        for j in range(8):
            r = lax.rsqrt(e[j, j])
            low = {i: e[i, j] * r for i in range(j + 1, 8)}
            for i in range(j + 1, 8):
                for k in range(j + 1, i + 1):
                    e[i, k] = e[i, k] - low[i] * low[k]
            left[j] = left[j] * r
            right[j] = right[j] * r
            for k in range(j):
                inv[j, k] = -(acc[j, k] * r)
            inv[j, j] = r
            for i in range(j + 1, 8):
                left[i] = left[i] - low[i] * left[j]
                right[i] = right[i] - low[i] * right[j]
                for k in range(j + 1):
                    t = low[i] * inv[j, k]
                    acc[i, k] = acc[i, k] + t if (i, k) in acc else t
        rows = right[0]
        for j in range(1, 8):
            rows = jnp.where(sub == j, right[j], rows)
        work[top : top + 8, 128:256] = rows
        if p == 15:
            break
        whole_left = []
        whole_right = []
        for i in range(8):
            a = inv[i, i] * left[i]
            b = inv[i, i] * right[i]
            for j in range(i + 1, 8):
                a = a + inv[j, i] * left[j]
                b = b + inv[j, i] * right[j]
            whole_left.append(a)
            whole_right.append(b)
        for q in range(top + 8, 128, 8):
            old = work[q : q + 8, 0:128]
            by = [lane_of(old, top + j) for j in range(8)]
            work[q : q + 8, 0:128] = old - total_of(by[j] * whole_left[j] for j in range(8))
            work[q : q + 8, 128:256] -= total_of(by[j] * whole_right[j] for j in range(8))


def stage(k, blocks, m, work, staged):
    eye = (
        lax.broadcasted_iota(jnp.int32, (128, 128), 0)
        == lax.broadcasted_iota(jnp.int32, (128, 128), 1)
    ).astype(F)
    base = pl.multiple_of(k * 128, 128)
    work[:, 0:128] = m[pl.ds(base, 128), pl.ds(base, 128)]
    work[:, 128:256] = eye
    leaf(work, staged)
    m[pl.ds(base, 128), pl.ds(base, 128)] = eye
    m[pl.ds(base, 128), :] = dot(work[:, 128:256], m[pl.ds(base, 128), :], 1, 0)

    def update(j, carry):
        at = pl.multiple_of(j * 128, 128)
        factor = m[pl.ds(base, 128), pl.ds(at, 128)]
        m[pl.ds(at, 128), pl.ds(base, 128)] = jnp.zeros((128, 128), F)
        m[pl.ds(at, 128), :] -= dot(factor, m[pl.ds(base, 128), :], 0, 0)
        return carry

    lax.fori_loop(k + 1, blocks, update, 0)


def factor_kernel(blocks, stages, gram_ref, m, work, staged):
    at = 0
    for r in range(blocks):
        for c in range(blocks):
            if c < r:
                m[r * 128 : (r + 1) * 128, c * 128 : (c + 1) * 128] = jnp.zeros((128, 128), F)
            else:
                m[r * 128 : (r + 1) * 128, c * 128 : (c + 1) * 128] = gram_ref[at : at + 128, :]
                at += 128

    def body(k, carry):
        stage(k, blocks, m, work, staged)
        return carry

    lax.fori_loop(0, stages, body, 0)


def apply_kernel(blocks, stages, scale, part_ref, sketch_ref, out_ref, m, work, staged):
    m[...] = part_ref[...]

    def body(k, carry):
        stage(k, blocks, m, work, staged)
        return carry

    lax.fori_loop(stages, blocks, body, 0)
    for r in range(blocks):
        for c in range(r + 1, blocks):
            m[r * 128 : (r + 1) * 128, c * 128 : (c + 1) * 128] = jnp.zeros((128, 128), F)
    inv_hi, inv_lo = split(m[...] * scale)

    def rows(i, carry):
        at = pl.multiple_of(i * 256, 256)
        hi, lo = split(sketch_ref[pl.ds(at, 256), :])
        out = dot(hi, inv_hi, 1, 1, None) + (dot(hi, inv_lo, 1, 1, None) + dot(lo, inv_hi, 1, 1, None))
        out_ref[pl.ds(at, 256), :] = out.astype(B)
        return carry

    lax.fori_loop(0, sketch_ref.shape[0] // 256, rows, 0)


FIRST = 3


def factored(gram_packed, rank):
    blocks = rank // 128
    return pl.pallas_call(
        functools.partial(factor_kernel, blocks, FIRST),
        out_shape=jax.ShapeDtypeStruct((rank, rank), F),
        in_specs=[VMEM],
        out_specs=VMEM,
        scratch_shapes=[pltpu.VMEM((128, 256), F), pltpu.VMEM((64, 128), F)],
        compiler_params=pltpu.CompilerParams(vmem_limit_bytes=LIMIT),
    )(gram_packed)


def applied(part, sketch, scale):
    rank = sketch.shape[1]
    return pl.pallas_call(
        functools.partial(apply_kernel, rank // 128, FIRST, scale),
        out_shape=jax.ShapeDtypeStruct(sketch.shape, B),
        in_specs=[VMEM] * 2,
        out_specs=VMEM,
        scratch_shapes=[
            pltpu.VMEM((rank, rank), F),
            pltpu.VMEM((128, 256), F),
            pltpu.VMEM((64, 128), F),
        ],
        compiler_params=pltpu.CompilerParams(vmem_limit_bytes=LIMIT),
    )(part, sketch)


def local(layer_input, conv_out, act_grad, conv_kernel, in_proj, sketch_matrix):
    conv, act, taps = conv_out[0], act_grad[0], conv_kernel[0]
    shards = lax.axis_size("seq")
    groups = lax.axis_size("tensor")
    count = lax.axis_size("pipe")
    rank = sketch_matrix.shape[-1]
    after = lax.ppermute(
        jnp.concatenate([conv[:8], act[:8]], axis=0),
        "seq",
        [(i + 1, i) for i in range(shards - 1)],
    )
    both = front(conv, act, taps, layer_input[0])
    gathered = lax.all_gather(both, "seq", axis=0)
    row_terms, edge = edge_and_rows(conv, act, after, taps, both, sketch_matrix[0])
    row_terms = lax.all_to_all(row_terms.reshape(groups, -1, rank), "tensor", 0, 0, tiled=True)
    rows = jnp.sum(row_terms, axis=0).astype(B)
    share = rows.shape[0]
    small = lax.all_gather(jnp.concatenate([rows, edge], axis=0), "seq", axis=0)
    rows, edges = small[:, :share], small[:, share:]
    rows = lax.all_to_all(
        jnp.broadcast_to(rows[None], (groups,) + rows.shape), "tensor", 0, 0, tiled=True
    )
    gathered, rows, edges = lax.optimization_barrier((gathered, rows, edges))
    sketch, gram, terms = middle(gathered, rows, edges, in_proj[0])
    input_grad = lax.psum_scatter(terms, "tensor", scatter_dimension=0, tiled=True)
    gram = lax.all_to_all(gram.reshape(groups, -1, 128), "tensor", 0, 0, tiled=True)
    gram = lax.all_gather(jnp.sum(gram, axis=0), "tensor", axis=0, tiled=True)
    part = factored(gram, rank)
    input_grad, part = lax.optimization_barrier((input_grad, part))
    passed = lax.ppermute(input_grad, "pipe", [(i, (i - 1) % count) for i in range(count)])
    basis = applied(part, sketch, math.sqrt(D))
    return (passed[None], basis[None])


def solution(mesh):
    placed = (
        P("pipe", "seq", "tensor"),
        P("pipe", "seq", "tensor"),
        P("pipe", "seq", "tensor"),
        P("pipe", None, "tensor"),
        P("pipe", "seq", "tensor"),
        P("pipe", "tensor", None),
    )
    return jax.shard_map(
        local,
        mesh=mesh,
        in_specs=placed,
        out_specs=(P("pipe", "tensor", "seq"), P("pipe", "tensor", None)),
        check_vma=False,
    )
```

```python
import functools
import math

import jax
import jax.numpy as jnp
from jax import lax
from jax.experimental import pallas as pl
from jax.experimental.pallas import tpu as pltpu
from jax.sharding import PartitionSpec as P

D = 8192
F = jnp.float32
B = jnp.bfloat16
HI = lax.Precision.HIGHEST
VMEM = pl.BlockSpec(memory_space=pltpu.VMEM)
ANY = pl.BlockSpec(memory_space=pl.ANY)
LIMIT = 32 * 1024 * 1024
WIDE = 58 * 1024 * 1024
MOST = 56 * 1024 * 1024
EDGE = 16


def dot(a, b, ca, cb, prec=HI):
    return lax.dot_general(
        a, b, (((ca,), (cb,)), ((), ())), precision=prec, preferred_element_type=F
    )


def split(x):
    hi = x.astype(B)
    return hi, (x - hi.astype(F)).astype(B)


def total_of(values):
    values = list(values)
    while len(values) > 1:
        values = [
            values[i] + values[i + 1] if i + 1 < len(values) else values[i]
            for i in range(0, len(values), 2)
        ]
    return values[0]


def pre_grad(p, g):
    sig = jax.nn.sigmoid(p)
    return g * sig * (1.0 + p * (1.0 - sig))


def convolved(held, taps, rows):
    total = taps[0:1, :] * held[0:rows, :]
    for tap in range(1, taps.shape[0]):
        total = total + taps[tap : tap + 1, :] * held[tap : tap + rows, :]
    return total.astype(B)


def front_kernel(conv_ref, act_ref, taps_ref, acts_ref, both_ref, held):
    rows = conv_ref.shape[0]
    held[0:rows, :] = pre_grad(conv_ref[...].astype(F), act_ref[...].astype(F))
    held[rows : rows + 8, :] = jnp.zeros((8, held.shape[1]), F)
    both_ref[0:rows, :] = acts_ref[...]
    both_ref[rows : 2 * rows, :] = convolved(held, taps_ref[...].astype(F), rows)


def front(conv, act, taps, acts):
    rows, width = conv.shape
    return pl.pallas_call(
        front_kernel,
        out_shape=jax.ShapeDtypeStruct((2 * rows, width), B),
        scratch_shapes=[pltpu.VMEM((rows + 8, width), F)],
        compiler_params=pltpu.CompilerParams(vmem_limit_bytes=WIDE),
    )(conv, act, taps, acts)


def edge_kernel(conv_ref, act_ref, next_ref, taps_ref, grad_ref, test_ref, rows_ref, edge_ref, held):
    held[0:EDGE, :] = pre_grad(conv_ref[...].astype(F), act_ref[...].astype(F))
    after = next_ref[...].astype(F)
    held[EDGE : EDGE + 8, :] = pre_grad(after[0:8, :], after[8:16, :])
    edge = convolved(held, taps_ref[...].astype(F), EDGE)
    half = edge.shape[1] // 2
    wide = edge.astype(F)
    edge_ref[...] = jnp.concatenate([wide[8:EDGE, half:], wide[8:EDGE, 0:half]], axis=0).astype(B)
    rows = grad_ref.shape[0]
    grad = jnp.concatenate([grad_ref[0 : rows - EDGE, :], edge], axis=0)
    rows_ref[...] = jnp.dot(grad, test_ref[...], preferred_element_type=F)


def edge_and_rows(conv, act, after, taps, both, test):
    rows, width = conv.shape
    rank = test.shape[1]
    last = rows // EDGE - 1

    def whole(*shape):
        return pl.BlockSpec(shape, lambda i: (0, 0))

    return pl.pallas_call(
        edge_kernel,
        grid=(1,),
        out_shape=(
            jax.ShapeDtypeStruct((rows, rank), F),
            jax.ShapeDtypeStruct((EDGE, width // 2), B),
        ),
        in_specs=[
            pl.BlockSpec((EDGE, width), lambda i: (last, 0)),
            pl.BlockSpec((EDGE, width), lambda i: (last, 0)),
            whole(*after.shape),
            whole(*taps.shape),
            pl.BlockSpec((rows, width), lambda i: (1, 0)),
            whole(*test.shape),
        ],
        out_specs=(whole(rows, rank), whole(EDGE, width // 2)),
        scratch_shapes=[pltpu.VMEM((EDGE + 8, width), F)],
        compiler_params=pltpu.CompilerParams(vmem_limit_bytes=WIDE),
    )(conv, act, after, taps, both, test)


def middle_kernel(
    both_ref, rows_ref, edge_ref, weight_ref, sketch_ref, gram_ref, terms_ref,
    acts, grads, terms, right, weights, sketch, gram, in_sems, out_sems,
):
    shards, twice, width = both_ref.shape
    tokens = twice // 2
    groups, _, share, rank = rows_ref.shape
    chunks, each = grads.shape[:2]
    cols = width // chunks

    def acts_copy(i):
        return pltpu.make_async_copy(
            both_ref.at[:, 0:tokens, i * cols : (i + 1) * cols], acts.at[i], in_sems.at[i]
        )

    def grads_copy(i):
        return pltpu.make_async_copy(
            both_ref.at[i * each : (i + 1) * each, tokens:twice, :], grads.at[i], in_sems.at[chunks + i]
        )

    def terms_copy(i):
        return pltpu.make_async_copy(
            terms.at[i], terms_ref.at[i * each * tokens : (i + 1) * each * tokens, :], out_sems.at[i]
        )

    def rows_copy(g):
        return pltpu.make_async_copy(
            rows_ref.at[g], right.at[:, g * share : (g + 1) * share, :], in_sems.at[2 * chunks + 1 + g]
        )

    def sketch_copy(i):
        at = slice(i * cols, (i + 1) * cols)
        return pltpu.make_async_copy(sketch.at[at, :], sketch_ref.at[at, :], out_sems.at[chunks + i])

    weight_copy = pltpu.make_async_copy(weight_ref, weights, in_sems.at[2 * chunks])
    gram_copy = pltpu.make_async_copy(gram, gram_ref, out_sems.at[2 * chunks])
    for g in range(groups):
        rows_copy(g).start()
    for i in range(chunks):
        acts_copy(i).start()
    weight_copy.start()
    for i in range(chunks):
        grads_copy(i).start()
    for g in range(groups):
        rows_copy(g).wait()
    for i in range(chunks):
        acts_copy(i).wait()
        left = acts[i].reshape(shards * tokens, cols)
        part = dot(left, right[...].reshape(shards * tokens, rank), 0, 0, None)
        sketch[i * cols : (i + 1) * cols, :] = part
        sketch_copy(i).start()
        at = 0
        for r in range(rank // 128):
            block = dot(part[:, r * 128 : (r + 1) * 128], part[:, r * 128 :], 0, 0)
            for c in range(block.shape[1] // 128):
                piece = block[:, c * 128 : (c + 1) * 128]
                if i == 0:
                    gram[at : at + 128, :] = piece
                else:
                    gram[at : at + 128, :] += piece
                at += 128
    gram_copy.start()
    half = width // 2
    final = lax.broadcasted_iota(jnp.int32, (EDGE, half), 0) >= 8
    weight_copy.wait()
    for i in range(chunks):
        grads_copy(i).wait()
        for z in range(each):
            edge = edge_ref[i * each + z].astype(F)
            other = jnp.concatenate([edge[8:EDGE, :], edge[0:8, :]], axis=0)
            old = grads[i, z, tokens - EDGE : tokens, :].astype(F)
            new = [jnp.where(final, edge, old[:, 0:half]), jnp.where(final, other, old[:, half:])]
            grads[i, z, tokens - EDGE : tokens, :] = jnp.concatenate(new, axis=1).astype(B)
        left = grads[i].reshape(each * tokens, width)
        terms[i] = dot(left, weights[...], 1, 1, None).astype(B)
        terms_copy(i).start()
    for i in range(chunks):
        sketch_copy(i).wait()
    gram_copy.wait()
    for i in range(chunks):
        terms_copy(i).wait()


def middle(gathered, rows, edges, weights):
    shards, twice, width = gathered.shape
    tokens = twice // 2
    rank = rows.shape[-1]
    blocks = rank // 128
    packed = blocks * (blocks + 1) // 2 * 128
    outs = weights.shape[0]
    chunks = 4
    each = shards // chunks
    return pl.pallas_call(
        middle_kernel,
        out_shape=(
            jax.ShapeDtypeStruct((width, rank), F),
            jax.ShapeDtypeStruct((packed, 128), F),
            jax.ShapeDtypeStruct((shards * tokens, outs), B),
        ),
        in_specs=[ANY, ANY, VMEM, ANY],
        out_specs=(ANY, ANY, ANY),
        scratch_shapes=[
            pltpu.VMEM((chunks, shards, tokens, width // chunks), B),
            pltpu.VMEM((chunks, each, tokens, width), B),
            pltpu.VMEM((chunks, each * tokens, outs), B),
            pltpu.VMEM((shards, tokens, rank), B),
            pltpu.VMEM(weights.shape, B),
            pltpu.VMEM((width, rank), F),
            pltpu.VMEM((packed, 128), F),
            pltpu.SemaphoreType.DMA((2 * chunks + 1 + rows.shape[0],)),
            pltpu.SemaphoreType.DMA((2 * chunks + 1,)),
        ],
        compiler_params=pltpu.CompilerParams(vmem_limit_bytes=MOST),
    )(gathered, rows, edges, weights)


def lane_of(x, l):
    return jnp.broadcast_to(x[:, l : l + 1], (8, 128))


def row_of(ref, r, c):
    return jnp.broadcast_to(ref[r : r + 1, c : c + 128], (8, 128))


def leaf(work, staged):
    sub = lax.broadcasted_iota(jnp.int32, (8, 128), 0)
    for p in range(16):
        top = 8 * p
        panel = work[top : top + 8, 0:128]
        left = [row_of(work, top + j, 0) for j in range(8)]
        right = [row_of(work, top + j, 128) for j in range(8)]
        e = {}
        for j in range(8):
            staged[8 * j : 8 * j + 8, :] = lane_of(panel, top + j)
            for i in range(j, 8):
                e[i, j] = row_of(staged, 8 * j + i, 0)
        inv = {}
        acc = {}
        for j in range(8):
            r = lax.rsqrt(e[j, j])
            low = {i: e[i, j] * r for i in range(j + 1, 8)}
            for i in range(j + 1, 8):
                for k in range(j + 1, i + 1):
                    e[i, k] = e[i, k] - low[i] * low[k]
            left[j] = left[j] * r
            right[j] = right[j] * r
            for k in range(j):
                inv[j, k] = -(acc[j, k] * r)
            inv[j, j] = r
            for i in range(j + 1, 8):
                left[i] = left[i] - low[i] * left[j]
                right[i] = right[i] - low[i] * right[j]
                for k in range(j + 1):
                    t = low[i] * inv[j, k]
                    acc[i, k] = acc[i, k] + t if (i, k) in acc else t
        rows = right[0]
        for j in range(1, 8):
            rows = jnp.where(sub == j, right[j], rows)
        work[top : top + 8, 128:256] = rows
        if p == 15:
            break
        whole_left = []
        whole_right = []
        for i in range(8):
            a = inv[i, i] * left[i]
            b = inv[i, i] * right[i]
            for j in range(i + 1, 8):
                a = a + inv[j, i] * left[j]
                b = b + inv[j, i] * right[j]
            whole_left.append(a)
            whole_right.append(b)
        for q in range(top + 8, 128, 8):
            old = work[q : q + 8, 0:128]
            by = [lane_of(old, top + j) for j in range(8)]
            work[q : q + 8, 0:128] = old - total_of(by[j] * whole_left[j] for j in range(8))
            work[q : q + 8, 128:256] -= total_of(by[j] * whole_right[j] for j in range(8))


def stage(k, blocks, m, work, staged):
    eye = (
        lax.broadcasted_iota(jnp.int32, (128, 128), 0)
        == lax.broadcasted_iota(jnp.int32, (128, 128), 1)
    ).astype(F)
    base = pl.multiple_of(k * 128, 128)
    work[:, 0:128] = m[pl.ds(base, 128), pl.ds(base, 128)]
    work[:, 128:256] = eye
    leaf(work, staged)
    m[pl.ds(base, 128), pl.ds(base, 128)] = eye
    m[pl.ds(base, 128), :] = dot(work[:, 128:256], m[pl.ds(base, 128), :], 1, 0)

    def update(j, carry):
        at = pl.multiple_of(j * 128, 128)
        factor = m[pl.ds(base, 128), pl.ds(at, 128)]
        m[pl.ds(at, 128), pl.ds(base, 128)] = jnp.zeros((128, 128), F)
        m[pl.ds(at, 128), :] -= dot(factor, m[pl.ds(base, 128), :], 0, 0)
        return carry

    lax.fori_loop(k + 1, blocks, update, 0)


def factor_kernel(blocks, stages, gram_ref, m, work, staged):
    at = 0
    for r in range(blocks):
        for c in range(blocks):
            if c < r:
                m[r * 128 : (r + 1) * 128, c * 128 : (c + 1) * 128] = jnp.zeros((128, 128), F)
            else:
                m[r * 128 : (r + 1) * 128, c * 128 : (c + 1) * 128] = gram_ref[at : at + 128, :]
                at += 128

    def body(k, carry):
        stage(k, blocks, m, work, staged)
        return carry

    lax.fori_loop(0, stages, body, 0)


def apply_kernel(blocks, stages, scale, part_ref, sketch_ref, out_ref, m, work, staged):
    m[...] = part_ref[...]

    def body(k, carry):
        stage(k, blocks, m, work, staged)
        return carry

    lax.fori_loop(stages, blocks, body, 0)
    for r in range(blocks):
        for c in range(r + 1, blocks):
            m[r * 128 : (r + 1) * 128, c * 128 : (c + 1) * 128] = jnp.zeros((128, 128), F)
    inv_hi, inv_lo = split(m[...] * scale)

    def rows(i, carry):
        at = pl.multiple_of(i * 256, 256)
        hi, lo = split(sketch_ref[pl.ds(at, 256), :])
        out = dot(hi, inv_hi, 1, 1, None) + (dot(hi, inv_lo, 1, 1, None) + dot(lo, inv_hi, 1, 1, None))
        out_ref[pl.ds(at, 256), :] = out.astype(B)
        return carry

    lax.fori_loop(0, sketch_ref.shape[0] // 256, rows, 0)


FIRST = 3


def factored(gram_packed, rank):
    blocks = rank // 128
    return pl.pallas_call(
        functools.partial(factor_kernel, blocks, FIRST),
        out_shape=jax.ShapeDtypeStruct((rank, rank), F),
        in_specs=[VMEM],
        out_specs=VMEM,
        scratch_shapes=[pltpu.VMEM((128, 256), F), pltpu.VMEM((64, 128), F)],
        compiler_params=pltpu.CompilerParams(vmem_limit_bytes=LIMIT),
    )(gram_packed)


def applied(part, sketch, scale):
    rank = sketch.shape[1]
    return pl.pallas_call(
        functools.partial(apply_kernel, rank // 128, FIRST, scale),
        out_shape=jax.ShapeDtypeStruct(sketch.shape, B),
        in_specs=[VMEM] * 2,
        out_specs=VMEM,
        scratch_shapes=[
            pltpu.VMEM((rank, rank), F),
            pltpu.VMEM((128, 256), F),
            pltpu.VMEM((64, 128), F),
        ],
        compiler_params=pltpu.CompilerParams(vmem_limit_bytes=LIMIT),
    )(part, sketch)


def local(layer_input, conv_out, act_grad, conv_kernel, in_proj, sketch_matrix):
    conv, act, taps = conv_out[0], act_grad[0], conv_kernel[0]
    shards = lax.axis_size("seq")
    groups = lax.axis_size("tensor")
    count = lax.axis_size("pipe")
    rank = sketch_matrix.shape[-1]
    after = lax.ppermute(
        jnp.concatenate([conv[:8], act[:8]], axis=0),
        "seq",
        [(i + 1, i) for i in range(shards - 1)],
    )
    both = front(conv, act, taps, layer_input[0])
    gathered = lax.all_gather(both, "seq", axis=0)
    row_terms, edge = edge_and_rows(conv, act, after, taps, both, sketch_matrix[0])
    row_terms = lax.all_to_all(row_terms.reshape(groups, -1, rank), "tensor", 0, 0, tiled=True)
    rows = jnp.sum(row_terms, axis=0).astype(B)
    share = rows.shape[0]
    small = lax.all_gather(jnp.concatenate([rows, edge], axis=0), "seq", axis=0)
    rows, edges = small[:, :share], small[:, share:]
    rows = lax.all_to_all(
        jnp.broadcast_to(rows[None], (groups,) + rows.shape), "tensor", 0, 0, tiled=True
    )
    gathered, rows, edges = lax.optimization_barrier((gathered, rows, edges))
    sketch, gram, terms = middle(gathered, rows, edges, in_proj[0])
    input_grad = lax.psum_scatter(terms, "tensor", scatter_dimension=0, tiled=True)
    gram = lax.all_to_all(gram.reshape(groups, -1, 128), "tensor", 0, 0, tiled=True)
    gram = lax.all_gather(jnp.sum(gram, axis=0), "tensor", axis=0, tiled=True)
    part = factored(gram, rank)
    input_grad, part = lax.optimization_barrier((input_grad, part))
    passed = lax.ppermute(input_grad, "pipe", [(i, (i - 1) % count) for i in range(count)])
    basis = applied(part, sketch, math.sqrt(D))
    return (passed[None], basis[None])


def solution(mesh):
    placed = (
        P("pipe", "seq", "tensor"),
        P("pipe", "seq", "tensor"),
        P("pipe", "seq", "tensor"),
        P("pipe", None, "tensor"),
        P("pipe", "seq", "tensor"),
        P("pipe", "tensor", None),
    )
    return jax.shard_map(
        local,
        mesh=mesh,
        in_specs=placed,
        out_specs=(P("pipe", "tensor", "seq"), P("pipe", "tensor", None)),
        check_vma=False,
    )
```

```python
import functools
import math

import jax
import jax.numpy as jnp
from jax import lax
from jax.experimental import pallas as pl
from jax.experimental.pallas import tpu as pltpu
from jax.sharding import PartitionSpec as P

D = 8192
F = jnp.float32
B = jnp.bfloat16
HI = lax.Precision.HIGHEST
VMEM = pl.BlockSpec(memory_space=pltpu.VMEM)
ANY = pl.BlockSpec(memory_space=pl.ANY)
LIMIT = 32 * 1024 * 1024
WIDE = 58 * 1024 * 1024
MOST = 56 * 1024 * 1024
EDGE = 16


def dot(a, b, ca, cb, prec=HI):
    return lax.dot_general(
        a, b, (((ca,), (cb,)), ((), ())), precision=prec, preferred_element_type=F
    )


def split(x):
    hi = x.astype(B)
    return hi, (x - hi.astype(F)).astype(B)


def total_of(values):
    values = list(values)
    while len(values) > 1:
        values = [
            values[i] + values[i + 1] if i + 1 < len(values) else values[i]
            for i in range(0, len(values), 2)
        ]
    return values[0]


def pre_grad(p, g):
    sig = jax.nn.sigmoid(p)
    return g * sig * (1.0 + p * (1.0 - sig))


def convolved(held, taps, rows):
    total = taps[0:1, :] * held[0:rows, :]
    for tap in range(1, taps.shape[0]):
        total = total + taps[tap : tap + 1, :] * held[tap : tap + rows, :]
    return total.astype(B)


def front_kernel(conv_ref, act_ref, taps_ref, acts_ref, both_ref, held):
    rows = conv_ref.shape[0]
    held[0:rows, :] = pre_grad(conv_ref[...].astype(F), act_ref[...].astype(F))
    held[rows : rows + 8, :] = jnp.zeros((8, held.shape[1]), F)
    both_ref[0:rows, :] = acts_ref[...]
    both_ref[rows : 2 * rows, :] = convolved(held, taps_ref[...].astype(F), rows)


def front(conv, act, taps, acts):
    rows, width = conv.shape
    part = width // 2

    def columns(count):
        return pl.BlockSpec((count, part), lambda i: (0, i))

    return pl.pallas_call(
        front_kernel,
        grid=(width // part,),
        out_shape=jax.ShapeDtypeStruct((2 * rows, width), B),
        in_specs=[columns(rows), columns(rows), columns(taps.shape[0]), columns(rows)],
        out_specs=columns(2 * rows),
        scratch_shapes=[pltpu.VMEM((rows + 8, part), F)],
        compiler_params=pltpu.CompilerParams(vmem_limit_bytes=WIDE),
    )(conv, act, taps, acts)


def edge_kernel(conv_ref, act_ref, next_ref, taps_ref, grad_ref, test_ref, rows_ref, edge_ref, held):
    held[0:EDGE, :] = pre_grad(conv_ref[...].astype(F), act_ref[...].astype(F))
    after = next_ref[...].astype(F)
    held[EDGE : EDGE + 8, :] = pre_grad(after[0:8, :], after[8:16, :])
    edge = convolved(held, taps_ref[...].astype(F), EDGE)
    half = edge.shape[1] // 2
    wide = edge.astype(F)
    edge_ref[...] = jnp.concatenate([wide[8:EDGE, half:], wide[8:EDGE, 0:half]], axis=0).astype(B)
    rows = grad_ref.shape[0]
    grad = jnp.concatenate([grad_ref[0 : rows - EDGE, :], edge], axis=0)
    rows_ref[...] = jnp.dot(grad, test_ref[...], preferred_element_type=F)


def edge_and_rows(conv, act, after, taps, both, test):
    rows, width = conv.shape
    rank = test.shape[1]
    last = rows // EDGE - 1

    def whole(*shape):
        return pl.BlockSpec(shape, lambda i: (0, 0))

    return pl.pallas_call(
        edge_kernel,
        grid=(1,),
        out_shape=(
            jax.ShapeDtypeStruct((rows, rank), F),
            jax.ShapeDtypeStruct((EDGE, width // 2), B),
        ),
        in_specs=[
            pl.BlockSpec((EDGE, width), lambda i: (last, 0)),
            pl.BlockSpec((EDGE, width), lambda i: (last, 0)),
            whole(*after.shape),
            whole(*taps.shape),
            pl.BlockSpec((rows, width), lambda i: (1, 0)),
            whole(*test.shape),
        ],
        out_specs=(whole(rows, rank), whole(EDGE, width // 2)),
        scratch_shapes=[pltpu.VMEM((EDGE + 8, width), F)],
        compiler_params=pltpu.CompilerParams(vmem_limit_bytes=WIDE),
    )(conv, act, after, taps, both, test)


def middle_kernel(
    both_ref, rows_ref, edge_ref, weight_ref, sketch_ref, gram_ref, terms_ref,
    acts, grads, terms, right, weights, sketch, gram, in_sems, out_sems,
):
    shards, twice, width = both_ref.shape
    tokens = twice // 2
    groups, _, share, rank = rows_ref.shape
    chunks, each = grads.shape[:2]
    cols = width // chunks

    def acts_copy(i):
        return pltpu.make_async_copy(
            both_ref.at[:, 0:tokens, i * cols : (i + 1) * cols], acts.at[i], in_sems.at[i]
        )

    def grads_copy(i):
        return pltpu.make_async_copy(
            both_ref.at[i * each : (i + 1) * each, tokens:twice, :], grads.at[i], in_sems.at[chunks + i]
        )

    def terms_copy(i):
        return pltpu.make_async_copy(
            terms.at[i], terms_ref.at[i * each * tokens : (i + 1) * each * tokens, :], out_sems.at[i]
        )

    def rows_copy(g):
        return pltpu.make_async_copy(
            rows_ref.at[g], right.at[:, g * share : (g + 1) * share, :], in_sems.at[2 * chunks + 1 + g]
        )

    def sketch_copy(i):
        at = slice(i * cols, (i + 1) * cols)
        return pltpu.make_async_copy(sketch.at[at, :], sketch_ref.at[at, :], out_sems.at[chunks + i])

    weight_copy = pltpu.make_async_copy(weight_ref, weights, in_sems.at[2 * chunks])
    gram_copy = pltpu.make_async_copy(gram, gram_ref, out_sems.at[2 * chunks])
    for g in range(groups):
        rows_copy(g).start()
    for i in range(chunks):
        acts_copy(i).start()
    weight_copy.start()
    for i in range(chunks):
        grads_copy(i).start()
    for g in range(groups):
        rows_copy(g).wait()
    for i in range(chunks):
        acts_copy(i).wait()
        left = acts[i].reshape(shards * tokens, cols)
        part = dot(left, right[...].reshape(shards * tokens, rank), 0, 0, None)
        sketch[i * cols : (i + 1) * cols, :] = part
        sketch_copy(i).start()
        at = 0
        for r in range(rank // 128):
            block = dot(part[:, r * 128 : (r + 1) * 128], part[:, r * 128 :], 0, 0)
            for c in range(block.shape[1] // 128):
                piece = block[:, c * 128 : (c + 1) * 128]
                if i == 0:
                    gram[at : at + 128, :] = piece
                else:
                    gram[at : at + 128, :] += piece
                at += 128
    gram_copy.start()
    half = width // 2
    final = lax.broadcasted_iota(jnp.int32, (EDGE, half), 0) >= 8
    weight_copy.wait()
    for i in range(chunks):
        grads_copy(i).wait()
        for z in range(each):
            edge = edge_ref[i * each + z].astype(F)
            other = jnp.concatenate([edge[8:EDGE, :], edge[0:8, :]], axis=0)
            old = grads[i, z, tokens - EDGE : tokens, :].astype(F)
            new = [jnp.where(final, edge, old[:, 0:half]), jnp.where(final, other, old[:, half:])]
            grads[i, z, tokens - EDGE : tokens, :] = jnp.concatenate(new, axis=1).astype(B)
        left = grads[i].reshape(each * tokens, width)
        terms[i] = dot(left, weights[...], 1, 1, None).astype(B)
        terms_copy(i).start()
    for i in range(chunks):
        sketch_copy(i).wait()
    gram_copy.wait()
    for i in range(chunks):
        terms_copy(i).wait()


def middle(gathered, rows, edges, weights):
    shards, twice, width = gathered.shape
    tokens = twice // 2
    rank = rows.shape[-1]
    blocks = rank // 128
    packed = blocks * (blocks + 1) // 2 * 128
    outs = weights.shape[0]
    chunks = 4
    each = shards // chunks
    return pl.pallas_call(
        middle_kernel,
        out_shape=(
            jax.ShapeDtypeStruct((width, rank), F),
            jax.ShapeDtypeStruct((packed, 128), F),
            jax.ShapeDtypeStruct((shards * tokens, outs), B),
        ),
        in_specs=[ANY, ANY, VMEM, ANY],
        out_specs=(ANY, ANY, ANY),
        scratch_shapes=[
            pltpu.VMEM((chunks, shards, tokens, width // chunks), B),
            pltpu.VMEM((chunks, each, tokens, width), B),
            pltpu.VMEM((chunks, each * tokens, outs), B),
            pltpu.VMEM((shards, tokens, rank), B),
            pltpu.VMEM(weights.shape, B),
            pltpu.VMEM((width, rank), F),
            pltpu.VMEM((packed, 128), F),
            pltpu.SemaphoreType.DMA((2 * chunks + 1 + rows.shape[0],)),
            pltpu.SemaphoreType.DMA((2 * chunks + 1,)),
        ],
        compiler_params=pltpu.CompilerParams(vmem_limit_bytes=MOST),
    )(gathered, rows, edges, weights)


def lane_of(x, l):
    return jnp.broadcast_to(x[:, l : l + 1], (8, 128))


def row_of(ref, r, c):
    return jnp.broadcast_to(ref[r : r + 1, c : c + 128], (8, 128))


def leaf(work, staged):
    sub = lax.broadcasted_iota(jnp.int32, (8, 128), 0)
    for p in range(16):
        top = 8 * p
        panel = work[top : top + 8, 0:128]
        left = [row_of(work, top + j, 0) for j in range(8)]
        right = [row_of(work, top + j, 128) for j in range(8)]
        e = {}
        for j in range(8):
            staged[8 * j : 8 * j + 8, :] = lane_of(panel, top + j)
            for i in range(j, 8):
                e[i, j] = row_of(staged, 8 * j + i, 0)
        inv = {}
        acc = {}
        for j in range(8):
            r = lax.rsqrt(e[j, j])
            low = {i: e[i, j] * r for i in range(j + 1, 8)}
            for i in range(j + 1, 8):
                for k in range(j + 1, i + 1):
                    e[i, k] = e[i, k] - low[i] * low[k]
            left[j] = left[j] * r
            right[j] = right[j] * r
            for k in range(j):
                inv[j, k] = -(acc[j, k] * r)
            inv[j, j] = r
            for i in range(j + 1, 8):
                left[i] = left[i] - low[i] * left[j]
                right[i] = right[i] - low[i] * right[j]
                for k in range(j + 1):
                    t = low[i] * inv[j, k]
                    acc[i, k] = acc[i, k] + t if (i, k) in acc else t
        rows = right[0]
        for j in range(1, 8):
            rows = jnp.where(sub == j, right[j], rows)
        work[top : top + 8, 128:256] = rows
        if p == 15:
            break
        whole_left = []
        whole_right = []
        for i in range(8):
            a = inv[i, i] * left[i]
            b = inv[i, i] * right[i]
            for j in range(i + 1, 8):
                a = a + inv[j, i] * left[j]
                b = b + inv[j, i] * right[j]
            whole_left.append(a)
            whole_right.append(b)
        for q in range(top + 8, 128, 8):
            old = work[q : q + 8, 0:128]
            by = [lane_of(old, top + j) for j in range(8)]
            work[q : q + 8, 0:128] = old - total_of(by[j] * whole_left[j] for j in range(8))
            work[q : q + 8, 128:256] -= total_of(by[j] * whole_right[j] for j in range(8))


def stage(k, blocks, m, work, staged):
    eye = (
        lax.broadcasted_iota(jnp.int32, (128, 128), 0)
        == lax.broadcasted_iota(jnp.int32, (128, 128), 1)
    ).astype(F)
    base = pl.multiple_of(k * 128, 128)
    work[:, 0:128] = m[pl.ds(base, 128), pl.ds(base, 128)]
    work[:, 128:256] = eye
    leaf(work, staged)
    width = blocks * 128

    def eliminate(top):
        end = top + 128
        inv = work[:, 128:256]
        if top > 0:
            m[top:end, 0:top] = dot(inv, m[top:end, 0:top], 1, 0)
        m[top:end, top:end] = inv
        if end < width:
            m[top:end, end:width] = dot(inv, m[top:end, end:width], 1, 0)
            change = dot(m[top:end, end:width], m[top:end, :], 0, 0)
            if top > 0:
                m[end:width, 0:top] -= change[:, 0:top]
            m[end:width, top:end] = -change[:, top:end]
            m[end:width, end:width] -= change[:, end:width]

    for which in range(blocks):
        pl.when(k == which)(functools.partial(eliminate, which * 128))


def factor_kernel(blocks, stages, gram_ref, m, work, staged):
    at = 0
    for r in range(blocks):
        for c in range(blocks):
            if c < r:
                m[r * 128 : (r + 1) * 128, c * 128 : (c + 1) * 128] = jnp.zeros((128, 128), F)
            else:
                m[r * 128 : (r + 1) * 128, c * 128 : (c + 1) * 128] = gram_ref[at : at + 128, :]
                at += 128

    def body(k, carry):
        stage(k, blocks, m, work, staged)
        return carry

    lax.fori_loop(0, stages, body, 0)


def apply_kernel(blocks, stages, scale, part_ref, sketch_ref, out_ref, m, work, staged):
    m[...] = part_ref[...]

    def body(k, carry):
        stage(k, blocks, m, work, staged)
        return carry

    lax.fori_loop(stages, blocks, body, 0)
    for r in range(blocks):
        for c in range(r + 1, blocks):
            m[r * 128 : (r + 1) * 128, c * 128 : (c + 1) * 128] = jnp.zeros((128, 128), F)
    rank = blocks * 128
    inv_hi, inv_lo = split(m[...] * scale)

    def rows(i, carry):
        at = pl.multiple_of(i * 256, 256)
        hi, lo = split(sketch_ref[pl.ds(at, 256), :])
        for c in range(0, rank, 256):
            end = min(c + 256, rank)
            left, right = inv_hi[c:end, 0:end], inv_lo[c:end, 0:end]
            out = dot(hi[:, 0:end], left, 1, 1, None)
            out += dot(hi[:, 0:end], right, 1, 1, None) + dot(lo[:, 0:end], left, 1, 1, None)
            out_ref[pl.ds(at, 256), c:end] = out.astype(B)
        return carry

    lax.fori_loop(0, sketch_ref.shape[0] // 256, rows, 0)


FIRST = 3


def factored(gram_packed, rank):
    blocks = rank // 128
    return pl.pallas_call(
        functools.partial(factor_kernel, blocks, FIRST),
        out_shape=jax.ShapeDtypeStruct((rank, rank), F),
        in_specs=[VMEM],
        out_specs=VMEM,
        scratch_shapes=[pltpu.VMEM((128, 256), F), pltpu.VMEM((64, 128), F)],
        compiler_params=pltpu.CompilerParams(vmem_limit_bytes=LIMIT),
    )(gram_packed)


def applied(part, sketch, scale):
    rank = sketch.shape[1]
    return pl.pallas_call(
        functools.partial(apply_kernel, rank // 128, FIRST, scale),
        out_shape=jax.ShapeDtypeStruct(sketch.shape, B),
        in_specs=[VMEM] * 2,
        out_specs=VMEM,
        scratch_shapes=[
            pltpu.VMEM((rank, rank), F),
            pltpu.VMEM((128, 256), F),
            pltpu.VMEM((64, 128), F),
        ],
        compiler_params=pltpu.CompilerParams(vmem_limit_bytes=LIMIT),
    )(part, sketch)


def local(layer_input, conv_out, act_grad, conv_kernel, in_proj, sketch_matrix):
    conv, act, taps = conv_out[0], act_grad[0], conv_kernel[0]
    shards = lax.axis_size("seq")
    groups = lax.axis_size("tensor")
    count = lax.axis_size("pipe")
    rank = sketch_matrix.shape[-1]
    after = lax.ppermute(
        jnp.concatenate([conv[:8], act[:8]], axis=0),
        "seq",
        [(i + 1, i) for i in range(shards - 1)],
    )
    both = front(conv, act, taps, layer_input[0])
    gathered = lax.all_gather(both, "seq", axis=0)
    row_terms, edge = edge_and_rows(conv, act, after, taps, both, sketch_matrix[0])
    row_terms = lax.all_to_all(row_terms.reshape(groups, -1, rank), "tensor", 0, 0, tiled=True)
    rows = jnp.sum(row_terms, axis=0).astype(B)
    share = rows.shape[0]
    small = lax.all_gather(jnp.concatenate([rows, edge], axis=0), "seq", axis=0)
    rows, edges = small[:, :share], small[:, share:]
    rows = lax.all_to_all(
        jnp.broadcast_to(rows[None], (groups,) + rows.shape), "tensor", 0, 0, tiled=True
    )
    gathered, rows, edges = lax.optimization_barrier((gathered, rows, edges))
    sketch, gram, terms = middle(gathered, rows, edges, in_proj[0])
    input_grad = lax.psum_scatter(terms, "tensor", scatter_dimension=0, tiled=True)
    gram = lax.all_to_all(gram.reshape(groups, -1, 128), "tensor", 0, 0, tiled=True)
    gram = lax.all_gather(jnp.sum(gram, axis=0), "tensor", axis=0, tiled=True)
    part = factored(gram, rank)
    input_grad, part = lax.optimization_barrier((input_grad, part))
    passed = lax.ppermute(input_grad, "pipe", [(i, (i - 1) % count) for i in range(count)])
    basis = applied(part, sketch, math.sqrt(D))
    return (passed[None], basis[None])


def solution(mesh):
    placed = (
        P("pipe", "seq", "tensor"),
        P("pipe", "seq", "tensor"),
        P("pipe", "seq", "tensor"),
        P("pipe", None, "tensor"),
        P("pipe", "seq", "tensor"),
        P("pipe", "tensor", None),
    )
    return jax.shard_map(
        local,
        mesh=mesh,
        in_specs=placed,
        out_specs=(P("pipe", "tensor", "seq"), P("pipe", "tensor", None)),
        check_vma=False,
    )
```

```python
import functools
import math

import jax
import jax.numpy as jnp
from jax import lax
from jax.experimental import pallas as pl
from jax.experimental.pallas import tpu as pltpu
from jax.sharding import PartitionSpec as P

D = 8192
F = jnp.float32
B = jnp.bfloat16
HI = lax.Precision.HIGHEST
VMEM = pl.BlockSpec(memory_space=pltpu.VMEM)
ANY = pl.BlockSpec(memory_space=pl.ANY)
LIMIT = 32 * 1024 * 1024
WIDE = 58 * 1024 * 1024
MOST = 56 * 1024 * 1024
EDGE = 16


def dot(a, b, ca, cb, prec=HI):
    return lax.dot_general(
        a, b, (((ca,), (cb,)), ((), ())), precision=prec, preferred_element_type=F
    )


def split(x):
    hi = x.astype(B)
    return hi, (x - hi.astype(F)).astype(B)


def total_of(values):
    values = list(values)
    while len(values) > 1:
        values = [
            values[i] + values[i + 1] if i + 1 < len(values) else values[i]
            for i in range(0, len(values), 2)
        ]
    return values[0]


def pre_grad(p, g):
    sig = jax.nn.sigmoid(p)
    return g * sig * (1.0 + p * (1.0 - sig))


def convolved(held, taps, rows):
    total = taps[0:1, :] * held[0:rows, :]
    for tap in range(1, taps.shape[0]):
        total = total + taps[tap : tap + 1, :] * held[tap : tap + rows, :]
    return total.astype(B)


def front_kernel(conv_ref, act_ref, taps_ref, acts_ref, both_ref, held):
    rows = conv_ref.shape[0]
    held[0:rows, :] = pre_grad(conv_ref[...].astype(F), act_ref[...].astype(F))
    held[rows : rows + 8, :] = jnp.zeros((8, held.shape[1]), F)
    both_ref[0:rows, :] = acts_ref[...]
    both_ref[rows : 2 * rows, :] = convolved(held, taps_ref[...].astype(F), rows)


def front(conv, act, taps, acts):
    rows, width = conv.shape
    part = width // 2

    def columns(count):
        return pl.BlockSpec((count, part), lambda i: (0, i))

    return pl.pallas_call(
        front_kernel,
        grid=(width // part,),
        out_shape=jax.ShapeDtypeStruct((2 * rows, width), B),
        in_specs=[columns(rows), columns(rows), columns(taps.shape[0]), columns(rows)],
        out_specs=columns(2 * rows),
        scratch_shapes=[pltpu.VMEM((rows + 8, part), F)],
        compiler_params=pltpu.CompilerParams(vmem_limit_bytes=WIDE),
    )(conv, act, taps, acts)


def edge_kernel(conv_ref, act_ref, next_ref, taps_ref, grad_ref, test_ref, rows_ref, edge_ref, held):
    held[0:EDGE, :] = pre_grad(conv_ref[...].astype(F), act_ref[...].astype(F))
    after = next_ref[...].astype(F)
    held[EDGE : EDGE + 8, :] = pre_grad(after[0:8, :], after[8:16, :])
    edge = convolved(held, taps_ref[...].astype(F), EDGE)
    quarter = edge.shape[1] // 4
    upper = lax.broadcasted_iota(jnp.int32, (8, quarter), 0) < 4
    last = edge.astype(F)[8:EDGE, :]
    last = [last[:, q * quarter : (q + 1) * quarter] for q in range(4)]
    pairs = [jnp.where(upper, pltpu.roll(last[q], 4, 0), last[q + 1]) for q in (0, 2)]
    edge_ref[...] = jnp.concatenate(pairs, axis=0).astype(B)
    rows = grad_ref.shape[0]
    grad = jnp.concatenate([grad_ref[0 : rows - EDGE, :], edge], axis=0)
    rows_ref[...] = jnp.dot(grad, test_ref[...], preferred_element_type=F)


def edge_and_rows(conv, act, after, taps, both, test):
    rows, width = conv.shape
    rank = test.shape[1]
    last = rows // EDGE - 1

    def whole(*shape):
        return pl.BlockSpec(shape, lambda i: (0, 0))

    return pl.pallas_call(
        edge_kernel,
        grid=(1,),
        out_shape=(
            jax.ShapeDtypeStruct((rows, rank), F),
            jax.ShapeDtypeStruct((EDGE, width // 4), B),
        ),
        in_specs=[
            pl.BlockSpec((EDGE, width), lambda i: (last, 0)),
            pl.BlockSpec((EDGE, width), lambda i: (last, 0)),
            whole(*after.shape),
            whole(*taps.shape),
            pl.BlockSpec((rows, width), lambda i: (1, 0)),
            whole(*test.shape),
        ],
        out_specs=(whole(rows, rank), whole(EDGE, width // 4)),
        scratch_shapes=[pltpu.VMEM((EDGE + 8, width), F)],
        compiler_params=pltpu.CompilerParams(vmem_limit_bytes=WIDE),
    )(conv, act, after, taps, both, test)


def middle_kernel(
    both_ref, rows_ref, edge_ref, weight_ref, sketch_ref, gram_ref, terms_ref,
    acts, grads, terms, right, weights, sketch, gram, in_sems, out_sems,
):
    shards, twice, width = both_ref.shape
    tokens = twice // 2
    groups, _, share, rank = rows_ref.shape
    chunks, each = grads.shape[:2]
    cols = width // chunks

    def acts_copy(i):
        return pltpu.make_async_copy(
            both_ref.at[:, 0:tokens, i * cols : (i + 1) * cols], acts.at[i], in_sems.at[i]
        )

    def grads_copy(i):
        return pltpu.make_async_copy(
            both_ref.at[i * each : (i + 1) * each, tokens:twice, :], grads.at[i], in_sems.at[chunks + i]
        )

    def terms_copy(i):
        return pltpu.make_async_copy(
            terms.at[i], terms_ref.at[i * each * tokens : (i + 1) * each * tokens, :], out_sems.at[i]
        )

    def rows_copy(g):
        return pltpu.make_async_copy(
            rows_ref.at[g], right.at[:, g * share : (g + 1) * share, :], in_sems.at[2 * chunks + 1 + g]
        )

    def sketch_copy(i):
        at = slice(i * cols, (i + 1) * cols)
        return pltpu.make_async_copy(sketch.at[at, :], sketch_ref.at[at, :], out_sems.at[chunks + i])

    weight_copy = pltpu.make_async_copy(weight_ref, weights, in_sems.at[2 * chunks])
    gram_copy = pltpu.make_async_copy(gram, gram_ref, out_sems.at[2 * chunks])
    for g in range(groups):
        rows_copy(g).start()
    for i in range(chunks):
        acts_copy(i).start()
    weight_copy.start()
    for i in range(chunks):
        grads_copy(i).start()
    for g in range(groups):
        rows_copy(g).wait()
    for i in range(chunks):
        acts_copy(i).wait()
        left = acts[i].reshape(shards * tokens, cols)
        part = dot(left, right[...].reshape(shards * tokens, rank), 0, 0, None)
        sketch[i * cols : (i + 1) * cols, :] = part
        sketch_copy(i).start()
        at = 0
        for r in range(rank // 128):
            block = dot(part[:, r * 128 : (r + 1) * 128], part[:, r * 128 :], 0, 0)
            for c in range(block.shape[1] // 128):
                piece = block[:, c * 128 : (c + 1) * 128]
                if i == 0:
                    gram[at : at + 128, :] = piece
                else:
                    gram[at : at + 128, :] += piece
                at += 128
    gram_copy.start()
    quarter = width // 4
    final = lax.broadcasted_iota(jnp.int32, (8, quarter), 0) >= 4
    weight_copy.wait()
    for i in range(chunks):
        grads_copy(i).wait()
        for z in range(each):
            edge = edge_ref[i * each + z].astype(F)
            old = grads[i, z, tokens - EDGE : tokens, :].astype(F)
            new = []
            for q in range(4):
                rows = edge[8 * (q // 2) : 8 * (q // 2) + 8, :]
                rows = rows if q % 2 else pltpu.roll(rows, 4, 0)
                new.append(jnp.where(final, rows, old[8:EDGE, q * quarter : (q + 1) * quarter]))
            new = jnp.concatenate([old[0:8, :], jnp.concatenate(new, axis=1)], axis=0)
            grads[i, z, tokens - EDGE : tokens, :] = new.astype(B)
        left = grads[i].reshape(each * tokens, width)
        terms[i] = dot(left, weights[...], 1, 1, None).astype(B)
        terms_copy(i).start()
    for i in range(chunks):
        sketch_copy(i).wait()
    gram_copy.wait()
    for i in range(chunks):
        terms_copy(i).wait()


def middle(gathered, rows, edges, weights):
    shards, twice, width = gathered.shape
    tokens = twice // 2
    rank = rows.shape[-1]
    blocks = rank // 128
    packed = blocks * (blocks + 1) // 2 * 128
    outs = weights.shape[0]
    chunks = 4
    each = shards // chunks
    return pl.pallas_call(
        middle_kernel,
        out_shape=(
            jax.ShapeDtypeStruct((width, rank), F),
            jax.ShapeDtypeStruct((packed, 128), F),
            jax.ShapeDtypeStruct((shards * tokens, outs), B),
        ),
        in_specs=[ANY, ANY, VMEM, ANY],
        out_specs=(ANY, ANY, ANY),
        scratch_shapes=[
            pltpu.VMEM((chunks, shards, tokens, width // chunks), B),
            pltpu.VMEM((chunks, each, tokens, width), B),
            pltpu.VMEM((chunks, each * tokens, outs), B),
            pltpu.VMEM((shards, tokens, rank), B),
            pltpu.VMEM(weights.shape, B),
            pltpu.VMEM((width, rank), F),
            pltpu.VMEM((packed, 128), F),
            pltpu.SemaphoreType.DMA((2 * chunks + 1 + rows.shape[0],)),
            pltpu.SemaphoreType.DMA((2 * chunks + 1,)),
        ],
        compiler_params=pltpu.CompilerParams(vmem_limit_bytes=MOST),
    )(gathered, rows, edges, weights)


def lane_of(x, l):
    return jnp.broadcast_to(x[:, l : l + 1], (8, 128))


def row_of(ref, r, c):
    return jnp.broadcast_to(ref[r : r + 1, c : c + 128], (8, 128))


def leaf(work, staged):
    sub = lax.broadcasted_iota(jnp.int32, (8, 128), 0)
    for p in range(16):
        top = 8 * p
        panel = work[top : top + 8, 0:128]
        left = [row_of(work, top + j, 0) for j in range(8)]
        right = [row_of(work, top + j, 128) for j in range(8)]
        e = {}
        for j in range(8):
            staged[8 * j : 8 * j + 8, :] = lane_of(panel, top + j)
            for i in range(j, 8):
                e[i, j] = row_of(staged, 8 * j + i, 0)
        inv = {}
        acc = {}
        for j in range(8):
            r = lax.rsqrt(e[j, j])
            low = {i: e[i, j] * r for i in range(j + 1, 8)}
            for i in range(j + 1, 8):
                for k in range(j + 1, i + 1):
                    e[i, k] = e[i, k] - low[i] * low[k]
            left[j] = left[j] * r
            right[j] = right[j] * r
            for k in range(j):
                inv[j, k] = -(acc[j, k] * r)
            inv[j, j] = r
            for i in range(j + 1, 8):
                left[i] = left[i] - low[i] * left[j]
                right[i] = right[i] - low[i] * right[j]
                for k in range(j + 1):
                    t = low[i] * inv[j, k]
                    acc[i, k] = acc[i, k] + t if (i, k) in acc else t
        rows = right[0]
        for j in range(1, 8):
            rows = jnp.where(sub == j, right[j], rows)
        work[top : top + 8, 128:256] = rows
        if p == 15:
            break
        whole_left = []
        whole_right = []
        for i in range(8):
            a = inv[i, i] * left[i]
            b = inv[i, i] * right[i]
            for j in range(i + 1, 8):
                a = a + inv[j, i] * left[j]
                b = b + inv[j, i] * right[j]
            whole_left.append(a)
            whole_right.append(b)
        for q in range(top + 8, 128, 8):
            old = work[q : q + 8, 0:128]
            by = [lane_of(old, top + j) for j in range(8)]
            work[q : q + 8, 0:128] = old - total_of(by[j] * whole_left[j] for j in range(8))
            work[q : q + 8, 128:256] -= total_of(by[j] * whole_right[j] for j in range(8))


def stage(k, blocks, m, work, staged):
    eye = (
        lax.broadcasted_iota(jnp.int32, (128, 128), 0)
        == lax.broadcasted_iota(jnp.int32, (128, 128), 1)
    ).astype(F)
    base = pl.multiple_of(k * 128, 128)
    work[:, 0:128] = m[pl.ds(base, 128), pl.ds(base, 128)]
    work[:, 128:256] = eye
    leaf(work, staged)
    width = blocks * 128

    def eliminate(top):
        end = top + 128
        inv = work[:, 128:256]
        if top > 0:
            m[top:end, 0:top] = dot(inv, m[top:end, 0:top], 1, 0)
        m[top:end, top:end] = inv
        if end < width:
            m[top:end, end:width] = dot(inv, m[top:end, end:width], 1, 0)
            change = dot(m[top:end, end:width], m[top:end, :], 0, 0)
            if top > 0:
                m[end:width, 0:top] -= change[:, 0:top]
            m[end:width, top:end] = -change[:, top:end]
            m[end:width, end:width] -= change[:, end:width]

    for which in range(blocks):
        pl.when(k == which)(functools.partial(eliminate, which * 128))


def factor_kernel(blocks, stages, gram_ref, m, work, staged):
    at = 0
    for r in range(blocks):
        for c in range(blocks):
            if c < r:
                m[r * 128 : (r + 1) * 128, c * 128 : (c + 1) * 128] = jnp.zeros((128, 128), F)
            else:
                m[r * 128 : (r + 1) * 128, c * 128 : (c + 1) * 128] = gram_ref[at : at + 128, :]
                at += 128

    def body(k, carry):
        stage(k, blocks, m, work, staged)
        return carry

    lax.fori_loop(0, stages, body, 0)


def apply_kernel(blocks, stages, scale, part_ref, sketch_ref, out_ref, m, work, staged):
    m[...] = part_ref[...]

    def body(k, carry):
        stage(k, blocks, m, work, staged)
        return carry

    lax.fori_loop(stages, blocks, body, 0)
    for r in range(blocks):
        for c in range(r + 1, blocks):
            m[r * 128 : (r + 1) * 128, c * 128 : (c + 1) * 128] = jnp.zeros((128, 128), F)
    rank = blocks * 128
    inv_hi, inv_lo = split(m[...] * scale)

    def rows(i, carry):
        at = pl.multiple_of(i * 256, 256)
        hi, lo = split(sketch_ref[pl.ds(at, 256), :])
        for c in range(0, rank, 256):
            end = min(c + 256, rank)
            left, right = inv_hi[c:end, 0:end], inv_lo[c:end, 0:end]
            out = dot(hi[:, 0:end], left, 1, 1, None)
            out += dot(hi[:, 0:end], right, 1, 1, None) + dot(lo[:, 0:end], left, 1, 1, None)
            out_ref[pl.ds(at, 256), c:end] = out.astype(B)
        return carry

    lax.fori_loop(0, sketch_ref.shape[0] // 256, rows, 0)


FIRST = 3


def factored(gram_packed, rank):
    blocks = rank // 128
    return pl.pallas_call(
        functools.partial(factor_kernel, blocks, FIRST),
        out_shape=jax.ShapeDtypeStruct((rank, rank), F),
        in_specs=[VMEM],
        out_specs=VMEM,
        scratch_shapes=[pltpu.VMEM((128, 256), F), pltpu.VMEM((64, 128), F)],
        compiler_params=pltpu.CompilerParams(vmem_limit_bytes=LIMIT),
    )(gram_packed)


def applied(part, sketch, scale):
    rank = sketch.shape[1]
    return pl.pallas_call(
        functools.partial(apply_kernel, rank // 128, FIRST, scale),
        out_shape=jax.ShapeDtypeStruct(sketch.shape, B),
        in_specs=[VMEM] * 2,
        out_specs=VMEM,
        scratch_shapes=[
            pltpu.VMEM((rank, rank), F),
            pltpu.VMEM((128, 256), F),
            pltpu.VMEM((64, 128), F),
        ],
        compiler_params=pltpu.CompilerParams(vmem_limit_bytes=LIMIT),
    )(part, sketch)


def local(layer_input, conv_out, act_grad, conv_kernel, in_proj, sketch_matrix):
    conv, act, taps = conv_out[0], act_grad[0], conv_kernel[0]
    shards = lax.axis_size("seq")
    groups = lax.axis_size("tensor")
    count = lax.axis_size("pipe")
    rank = sketch_matrix.shape[-1]
    after = lax.ppermute(
        jnp.concatenate([conv[:8], act[:8]], axis=0),
        "seq",
        [(i + 1, i) for i in range(shards - 1)],
    )
    both = front(conv, act, taps, layer_input[0])
    gathered = lax.all_gather(both, "seq", axis=0)
    row_terms, edge = edge_and_rows(conv, act, after, taps, both, sketch_matrix[0])
    row_terms = lax.all_to_all(row_terms.reshape(groups, -1, rank), "tensor", 0, 0, tiled=True)
    rows = jnp.sum(row_terms, axis=0).astype(B)
    small = lax.all_gather(jnp.concatenate([rows, edge], axis=1), "seq", axis=0)
    rows, edges = small[:, :, :rank], small[:, :, rank:]
    rows = lax.all_to_all(
        jnp.broadcast_to(rows[None], (groups,) + rows.shape), "tensor", 0, 0, tiled=True
    )
    gathered, rows, edges = lax.optimization_barrier((gathered, rows, edges))
    sketch, gram, terms = middle(gathered, rows, edges, in_proj[0])
    input_grad = lax.psum_scatter(terms, "tensor", scatter_dimension=0, tiled=True)
    gram = lax.all_to_all(gram.reshape(groups, -1, 128), "tensor", 0, 0, tiled=True)
    gram = lax.all_gather(jnp.sum(gram, axis=0), "tensor", axis=0, tiled=True)
    part = factored(gram, rank)
    input_grad, part = lax.optimization_barrier((input_grad, part))
    passed = lax.ppermute(input_grad, "pipe", [(i, (i - 1) % count) for i in range(count)])
    basis = applied(part, sketch, math.sqrt(D))
    return (passed[None], basis[None])


def solution(mesh):
    placed = (
        P("pipe", "seq", "tensor"),
        P("pipe", "seq", "tensor"),
        P("pipe", "seq", "tensor"),
        P("pipe", None, "tensor"),
        P("pipe", "seq", "tensor"),
        P("pipe", "tensor", None),
    )
    return jax.shard_map(
        local,
        mesh=mesh,
        in_specs=placed,
        out_specs=(P("pipe", "tensor", "seq"), P("pipe", "tensor", None)),
        check_vma=False,
    )
```

```python
import functools
import math

import jax
import jax.numpy as jnp
from jax import lax
from jax.experimental import pallas as pl
from jax.experimental.pallas import tpu as pltpu
from jax.sharding import PartitionSpec as P

D = 8192
F = jnp.float32
B = jnp.bfloat16
HI = lax.Precision.HIGHEST
VMEM = pl.BlockSpec(memory_space=pltpu.VMEM)
ANY = pl.BlockSpec(memory_space=pl.ANY)
LIMIT = 32 * 1024 * 1024
WIDE = 58 * 1024 * 1024
MOST = 56 * 1024 * 1024
EDGE = 16


def dot(a, b, ca, cb, prec=HI):
    return lax.dot_general(
        a, b, (((ca,), (cb,)), ((), ())), precision=prec, preferred_element_type=F
    )


def split(x):
    hi = x.astype(B)
    return hi, (x - hi.astype(F)).astype(B)


def total_of(values):
    values = list(values)
    while len(values) > 1:
        values = [
            values[i] + values[i + 1] if i + 1 < len(values) else values[i]
            for i in range(0, len(values), 2)
        ]
    return values[0]


def pre_grad(p, g):
    sig = jax.nn.sigmoid(p)
    return g * sig * (1.0 + p * (1.0 - sig))


def convolved(held, taps, rows):
    total = taps[0:1, :] * held[0:rows, :]
    for tap in range(1, taps.shape[0]):
        total = total + taps[tap : tap + 1, :] * held[tap : tap + rows, :]
    return total.astype(B)


def front_kernel(conv_ref, act_ref, taps_ref, acts_ref, both_ref, held):
    rows = conv_ref.shape[0]
    held[0:rows, :] = pre_grad(conv_ref[...].astype(F), act_ref[...].astype(F))
    held[rows : rows + 8, :] = jnp.zeros((8, held.shape[1]), F)
    both_ref[0:rows, :] = acts_ref[...]
    both_ref[rows : 2 * rows, :] = convolved(held, taps_ref[...].astype(F), rows)


def front(conv, act, taps, acts):
    rows, width = conv.shape
    part = width // 2

    def columns(count):
        return pl.BlockSpec((count, part), lambda i: (0, i))

    return pl.pallas_call(
        front_kernel,
        grid=(width // part,),
        out_shape=jax.ShapeDtypeStruct((2 * rows, width), B),
        in_specs=[columns(rows), columns(rows), columns(taps.shape[0]), columns(rows)],
        out_specs=columns(2 * rows),
        scratch_shapes=[pltpu.VMEM((rows + 8, part), F)],
        compiler_params=pltpu.CompilerParams(vmem_limit_bytes=WIDE),
    )(conv, act, taps, acts)


def edge_kernel(conv_ref, act_ref, next_ref, taps_ref, grad_ref, test_ref, rows_ref, edge_ref, held):
    held[0:EDGE, :] = pre_grad(conv_ref[...].astype(F), act_ref[...].astype(F))
    after = next_ref[...].astype(F)
    held[EDGE : EDGE + 8, :] = pre_grad(after[0:8, :], after[8:16, :])
    edge = convolved(held, taps_ref[...].astype(F), EDGE)
    quarter = edge.shape[1] // 4
    upper = lax.broadcasted_iota(jnp.int32, (8, quarter), 0) < 4
    last = edge.astype(F)[8:EDGE, :]
    last = [last[:, q * quarter : (q + 1) * quarter] for q in range(4)]
    pairs = [jnp.where(upper, pltpu.roll(last[q], 4, 0), last[q + 1]) for q in (0, 2)]
    edge_ref[...] = jnp.concatenate(pairs, axis=0).astype(B)
    rows = grad_ref.shape[0]
    grad = jnp.concatenate([grad_ref[0 : rows - EDGE, :], edge], axis=0)
    rows_ref[...] = jnp.dot(grad, test_ref[...], preferred_element_type=F)


def edge_and_rows(conv, act, after, taps, both, test):
    rows, width = conv.shape
    rank = test.shape[1]
    last = rows // EDGE - 1

    def whole(*shape):
        return pl.BlockSpec(shape, lambda i: (0, 0))

    return pl.pallas_call(
        edge_kernel,
        grid=(1,),
        out_shape=(
            jax.ShapeDtypeStruct((rows, rank), F),
            jax.ShapeDtypeStruct((EDGE, width // 4), B),
        ),
        in_specs=[
            pl.BlockSpec((EDGE, width), lambda i: (last, 0)),
            pl.BlockSpec((EDGE, width), lambda i: (last, 0)),
            whole(*after.shape),
            whole(*taps.shape),
            pl.BlockSpec((rows, width), lambda i: (1, 0)),
            whole(*test.shape),
        ],
        out_specs=(whole(rows, rank), whole(EDGE, width // 4)),
        scratch_shapes=[pltpu.VMEM((EDGE + 8, width), F)],
        compiler_params=pltpu.CompilerParams(vmem_limit_bytes=WIDE),
    )(conv, act, after, taps, both, test)


def middle_kernel(
    both_ref, rows_ref, edge_ref, weight_ref, sketch_ref, gram_ref, terms_ref,
    acts, grads, terms, right, weights, sketch, gram, in_sems, out_sems,
):
    shards, twice, width = both_ref.shape
    tokens = twice // 2
    groups, _, share, rank = rows_ref.shape
    chunks, each = grads.shape[:2]
    cols = width // chunks

    def acts_copy(i):
        return pltpu.make_async_copy(
            both_ref.at[:, 0:tokens, i * cols : (i + 1) * cols], acts.at[i], in_sems.at[i]
        )

    def grads_copy(i):
        return pltpu.make_async_copy(
            both_ref.at[i * each : (i + 1) * each, tokens:twice, :], grads.at[i], in_sems.at[chunks + i]
        )

    def terms_copy(i):
        return pltpu.make_async_copy(
            terms.at[i], terms_ref.at[i * each * tokens : (i + 1) * each * tokens, :], out_sems.at[i]
        )

    def rows_copy(g):
        return pltpu.make_async_copy(
            rows_ref.at[g], right.at[:, g * share : (g + 1) * share, :], in_sems.at[2 * chunks + 1 + g]
        )

    def sketch_copy(i):
        at = slice(i * cols, (i + 1) * cols)
        return pltpu.make_async_copy(sketch.at[at, :], sketch_ref.at[at, :], out_sems.at[chunks + i])

    weight_copy = pltpu.make_async_copy(weight_ref, weights, in_sems.at[2 * chunks])
    gram_copy = pltpu.make_async_copy(gram, gram_ref, out_sems.at[2 * chunks])
    for g in range(groups):
        rows_copy(g).start()
    for i in range(chunks):
        acts_copy(i).start()
    weight_copy.start()
    for i in range(chunks):
        grads_copy(i).start()
    for g in range(groups):
        rows_copy(g).wait()
    for i in range(chunks):
        acts_copy(i).wait()
        left = acts[i].reshape(shards * tokens, cols)
        part = dot(left, right[...].reshape(shards * tokens, rank), 0, 0, None)
        sketch[i * cols : (i + 1) * cols, :] = part
        sketch_copy(i).start()
        at = 0
        for r in range(rank // 128):
            block = dot(part[:, r * 128 : (r + 1) * 128], part[:, r * 128 :], 0, 0)
            for c in range(block.shape[1] // 128):
                piece = block[:, c * 128 : (c + 1) * 128]
                if i == 0:
                    gram[at : at + 128, :] = piece
                else:
                    gram[at : at + 128, :] += piece
                at += 128
    gram_copy.start()
    quarter = width // 4
    final = lax.broadcasted_iota(jnp.int32, (8, quarter), 0) >= 4
    weight_copy.wait()
    for i in range(chunks):
        grads_copy(i).wait()
        for z in range(each):
            edge = edge_ref[i * each + z].astype(F)
            old = grads[i, z, tokens - EDGE : tokens, :].astype(F)
            new = []
            for q in range(4):
                rows = edge[8 * (q // 2) : 8 * (q // 2) + 8, :]
                rows = rows if q % 2 else pltpu.roll(rows, 4, 0)
                new.append(jnp.where(final, rows, old[8:EDGE, q * quarter : (q + 1) * quarter]))
            new = jnp.concatenate([old[0:8, :], jnp.concatenate(new, axis=1)], axis=0)
            grads[i, z, tokens - EDGE : tokens, :] = new.astype(B)
        left = grads[i].reshape(each * tokens, width)
        terms[i] = dot(left, weights[...], 1, 1, None).astype(B)
        terms_copy(i).start()
    for i in range(chunks):
        sketch_copy(i).wait()
    gram_copy.wait()
    for i in range(chunks):
        terms_copy(i).wait()


def middle(gathered, rows, edges, weights):
    shards, twice, width = gathered.shape
    tokens = twice // 2
    rank = rows.shape[-1]
    blocks = rank // 128
    packed = blocks * (blocks + 1) // 2 * 128
    outs = weights.shape[0]
    chunks = 2
    each = shards // chunks
    return pl.pallas_call(
        middle_kernel,
        out_shape=(
            jax.ShapeDtypeStruct((width, rank), F),
            jax.ShapeDtypeStruct((packed, 128), F),
            jax.ShapeDtypeStruct((shards * tokens, outs), B),
        ),
        in_specs=[ANY, ANY, VMEM, ANY],
        out_specs=(ANY, ANY, ANY),
        scratch_shapes=[
            pltpu.VMEM((chunks, shards, tokens, width // chunks), B),
            pltpu.VMEM((chunks, each, tokens, width), B),
            pltpu.VMEM((chunks, each * tokens, outs), B),
            pltpu.VMEM((shards, tokens, rank), B),
            pltpu.VMEM(weights.shape, B),
            pltpu.VMEM((width, rank), F),
            pltpu.VMEM((packed, 128), F),
            pltpu.SemaphoreType.DMA((2 * chunks + 1 + rows.shape[0],)),
            pltpu.SemaphoreType.DMA((2 * chunks + 1,)),
        ],
        compiler_params=pltpu.CompilerParams(vmem_limit_bytes=MOST),
    )(gathered, rows, edges, weights)


def lane_of(x, l):
    return jnp.broadcast_to(x[:, l : l + 1], (8, 128))


def row_of(ref, r, c):
    return jnp.broadcast_to(ref[r : r + 1, c : c + 128], (8, 128))


def leaf(work, staged):
    sub = lax.broadcasted_iota(jnp.int32, (8, 128), 0)
    for p in range(16):
        top = 8 * p
        panel = work[top : top + 8, 0:128]
        left = [row_of(work, top + j, 0) for j in range(8)]
        right = [row_of(work, top + j, 128) for j in range(8)]
        e = {}
        for j in range(8):
            staged[8 * j : 8 * j + 8, :] = lane_of(panel, top + j)
            for i in range(j, 8):
                e[i, j] = row_of(staged, 8 * j + i, 0)
        inv = {}
        acc = {}
        for j in range(8):
            r = lax.rsqrt(e[j, j])
            low = {i: e[i, j] * r for i in range(j + 1, 8)}
            for i in range(j + 1, 8):
                for k in range(j + 1, i + 1):
                    e[i, k] = e[i, k] - low[i] * low[k]
            left[j] = left[j] * r
            right[j] = right[j] * r
            for k in range(j):
                inv[j, k] = -(acc[j, k] * r)
            inv[j, j] = r
            for i in range(j + 1, 8):
                left[i] = left[i] - low[i] * left[j]
                right[i] = right[i] - low[i] * right[j]
                for k in range(j + 1):
                    t = low[i] * inv[j, k]
                    acc[i, k] = acc[i, k] + t if (i, k) in acc else t
        rows = right[0]
        for j in range(1, 8):
            rows = jnp.where(sub == j, right[j], rows)
        work[top : top + 8, 128:256] = rows
        if p == 15:
            break
        whole_left = []
        whole_right = []
        for i in range(8):
            a = inv[i, i] * left[i]
            b = inv[i, i] * right[i]
            for j in range(i + 1, 8):
                a = a + inv[j, i] * left[j]
                b = b + inv[j, i] * right[j]
            whole_left.append(a)
            whole_right.append(b)
        for q in range(top + 8, 128, 8):
            old = work[q : q + 8, 0:128]
            by = [lane_of(old, top + j) for j in range(8)]
            work[q : q + 8, 0:128] = old - total_of(by[j] * whole_left[j] for j in range(8))
            work[q : q + 8, 128:256] -= total_of(by[j] * whole_right[j] for j in range(8))


def stage(k, blocks, m, work, staged):
    eye = (
        lax.broadcasted_iota(jnp.int32, (128, 128), 0)
        == lax.broadcasted_iota(jnp.int32, (128, 128), 1)
    ).astype(F)
    base = pl.multiple_of(k * 128, 128)
    work[:, 0:128] = m[pl.ds(base, 128), pl.ds(base, 128)]
    work[:, 128:256] = eye
    leaf(work, staged)
    width = blocks * 128

    def eliminate(top):
        end = top + 128
        inv = work[:, 128:256]
        if top > 0:
            m[top:end, 0:top] = dot(inv, m[top:end, 0:top], 1, 0)
        m[top:end, top:end] = inv
        if end < width:
            m[top:end, end:width] = dot(inv, m[top:end, end:width], 1, 0)
            change = dot(m[top:end, end:width], m[top:end, :], 0, 0)
            if top > 0:
                m[end:width, 0:top] -= change[:, 0:top]
            m[end:width, top:end] = -change[:, top:end]
            m[end:width, end:width] -= change[:, end:width]

    for which in range(blocks):
        pl.when(k == which)(functools.partial(eliminate, which * 128))


def factor_kernel(blocks, stages, gram_ref, m, work, staged):
    at = 0
    for r in range(blocks):
        for c in range(blocks):
            if c < r:
                m[r * 128 : (r + 1) * 128, c * 128 : (c + 1) * 128] = jnp.zeros((128, 128), F)
            else:
                m[r * 128 : (r + 1) * 128, c * 128 : (c + 1) * 128] = gram_ref[at : at + 128, :]
                at += 128

    def body(k, carry):
        stage(k, blocks, m, work, staged)
        return carry

    lax.fori_loop(0, stages, body, 0)


def apply_kernel(blocks, stages, scale, part_ref, sketch_ref, out_ref, m, work, staged):
    m[...] = part_ref[...]

    def body(k, carry):
        stage(k, blocks, m, work, staged)
        return carry

    lax.fori_loop(stages, blocks, body, 0)
    for r in range(blocks):
        for c in range(r + 1, blocks):
            m[r * 128 : (r + 1) * 128, c * 128 : (c + 1) * 128] = jnp.zeros((128, 128), F)
    rank = blocks * 128
    inv_hi, inv_lo = split(m[...] * scale)

    def rows(i, carry):
        at = pl.multiple_of(i * 256, 256)
        hi, lo = split(sketch_ref[pl.ds(at, 256), :])
        for c in range(0, rank, 256):
            end = min(c + 256, rank)
            left, right = inv_hi[c:end, 0:end], inv_lo[c:end, 0:end]
            out = dot(hi[:, 0:end], left, 1, 1, None)
            out += dot(hi[:, 0:end], right, 1, 1, None) + dot(lo[:, 0:end], left, 1, 1, None)
            out_ref[pl.ds(at, 256), c:end] = out.astype(B)
        return carry

    lax.fori_loop(0, sketch_ref.shape[0] // 256, rows, 0)


FIRST = 3


def factored(gram_packed, rank):
    blocks = rank // 128
    return pl.pallas_call(
        functools.partial(factor_kernel, blocks, FIRST),
        out_shape=jax.ShapeDtypeStruct((rank, rank), F),
        in_specs=[VMEM],
        out_specs=VMEM,
        scratch_shapes=[pltpu.VMEM((128, 256), F), pltpu.VMEM((64, 128), F)],
        compiler_params=pltpu.CompilerParams(vmem_limit_bytes=LIMIT),
    )(gram_packed)


def applied(part, sketch, scale):
    rank = sketch.shape[1]
    return pl.pallas_call(
        functools.partial(apply_kernel, rank // 128, FIRST, scale),
        out_shape=jax.ShapeDtypeStruct(sketch.shape, B),
        in_specs=[VMEM] * 2,
        out_specs=VMEM,
        scratch_shapes=[
            pltpu.VMEM((rank, rank), F),
            pltpu.VMEM((128, 256), F),
            pltpu.VMEM((64, 128), F),
        ],
        compiler_params=pltpu.CompilerParams(vmem_limit_bytes=LIMIT),
    )(part, sketch)


def local(layer_input, conv_out, act_grad, conv_kernel, in_proj, sketch_matrix):
    conv, act, taps = conv_out[0], act_grad[0], conv_kernel[0]
    shards = lax.axis_size("seq")
    groups = lax.axis_size("tensor")
    count = lax.axis_size("pipe")
    rank = sketch_matrix.shape[-1]
    after = lax.ppermute(
        jnp.concatenate([conv[:8], act[:8]], axis=0),
        "seq",
        [(i + 1, i) for i in range(shards - 1)],
    )
    both = front(conv, act, taps, layer_input[0])
    gathered = lax.all_gather(both, "seq", axis=0)
    row_terms, edge = edge_and_rows(conv, act, after, taps, both, sketch_matrix[0])
    row_terms = lax.all_to_all(row_terms.reshape(groups, -1, rank), "tensor", 0, 0, tiled=True)
    rows = jnp.sum(row_terms, axis=0).astype(B)
    small = lax.all_gather(jnp.concatenate([rows, edge], axis=1), "seq", axis=0)
    rows, edges = small[:, :, :rank], small[:, :, rank:]
    rows = lax.all_to_all(
        jnp.broadcast_to(rows[None], (groups,) + rows.shape), "tensor", 0, 0, tiled=True
    )
    gathered, rows, edges = lax.optimization_barrier((gathered, rows, edges))
    sketch, gram, terms = middle(gathered, rows, edges, in_proj[0])
    input_grad = lax.psum_scatter(terms, "tensor", scatter_dimension=0, tiled=True)
    gram = lax.all_to_all(gram.reshape(groups, -1, 128), "tensor", 0, 0, tiled=True)
    gram = lax.all_gather(jnp.sum(gram, axis=0), "tensor", axis=0, tiled=True)
    part = factored(gram, rank)
    input_grad, part = lax.optimization_barrier((input_grad, part))
    passed = lax.ppermute(input_grad, "pipe", [(i, (i - 1) % count) for i in range(count)])
    basis = applied(part, sketch, math.sqrt(D))
    return (passed[None], basis[None])


def solution(mesh):
    placed = (
        P("pipe", "seq", "tensor"),
        P("pipe", "seq", "tensor"),
        P("pipe", "seq", "tensor"),
        P("pipe", None, "tensor"),
        P("pipe", "seq", "tensor"),
        P("pipe", "tensor", None),
    )
    return jax.shard_map(
        local,
        mesh=mesh,
        in_specs=placed,
        out_specs=(P("pipe", "tensor", "seq"), P("pipe", "tensor", None)),
        check_vma=False,
    )
```

```python
import functools
import math

import jax
import jax.numpy as jnp
from jax import lax
from jax.experimental import pallas as pl
from jax.experimental.pallas import tpu as pltpu
from jax.sharding import PartitionSpec as P

D = 8192
F = jnp.float32
B = jnp.bfloat16
HI = lax.Precision.HIGHEST
VMEM = pl.BlockSpec(memory_space=pltpu.VMEM)
ANY = pl.BlockSpec(memory_space=pl.ANY)
LIMIT = 32 * 1024 * 1024
WIDE = 58 * 1024 * 1024
MOST = 56 * 1024 * 1024
EDGE = 16


def dot(a, b, ca, cb, prec=HI):
    return lax.dot_general(
        a, b, (((ca,), (cb,)), ((), ())), precision=prec, preferred_element_type=F
    )


def split(x):
    hi = x.astype(B)
    return hi, (x - hi.astype(F)).astype(B)


def total_of(values):
    values = list(values)
    while len(values) > 1:
        values = [
            values[i] + values[i + 1] if i + 1 < len(values) else values[i]
            for i in range(0, len(values), 2)
        ]
    return values[0]


def pre_grad(p, g):
    sig = jax.nn.sigmoid(p)
    return g * sig * (1.0 + p * (1.0 - sig))


def convolved(held, taps, rows):
    total = taps[0:1, :] * held[0:rows, :]
    for tap in range(1, taps.shape[0]):
        total = total + taps[tap : tap + 1, :] * held[tap : tap + rows, :]
    return total.astype(B)


def front_kernel(conv_ref, act_ref, taps_ref, acts_ref, both_ref, held):
    rows = conv_ref.shape[0]
    held[0:rows, :] = pre_grad(conv_ref[...].astype(F), act_ref[...].astype(F))
    held[rows : rows + 8, :] = jnp.zeros((8, held.shape[1]), F)
    both_ref[0:rows, :] = acts_ref[...]
    both_ref[rows : 2 * rows, :] = convolved(held, taps_ref[...].astype(F), rows)


def front(conv, act, taps, acts):
    rows, width = conv.shape
    part = width // 2

    def columns(count):
        return pl.BlockSpec((count, part), lambda i: (0, i))

    return pl.pallas_call(
        front_kernel,
        grid=(width // part,),
        out_shape=jax.ShapeDtypeStruct((2 * rows, width), B),
        in_specs=[columns(rows), columns(rows), columns(taps.shape[0]), columns(rows)],
        out_specs=columns(2 * rows),
        scratch_shapes=[pltpu.VMEM((rows + 8, part), F)],
        compiler_params=pltpu.CompilerParams(vmem_limit_bytes=WIDE),
    )(conv, act, taps, acts)


def edge_kernel(conv_ref, act_ref, next_ref, taps_ref, grad_ref, test_ref, rows_ref, edge_ref, held):
    held[0:EDGE, :] = pre_grad(conv_ref[...].astype(F), act_ref[...].astype(F))
    after = next_ref[...].astype(F)
    held[EDGE : EDGE + 8, :] = pre_grad(after[0:8, :], after[8:16, :])
    edge = convolved(held, taps_ref[...].astype(F), EDGE)
    quarter = edge.shape[1] // 4
    upper = lax.broadcasted_iota(jnp.int32, (8, quarter), 0) < 4
    last = edge.astype(F)[8:EDGE, :]
    last = [last[:, q * quarter : (q + 1) * quarter] for q in range(4)]
    pairs = [jnp.where(upper, pltpu.roll(last[q], 4, 0), last[q + 1]) for q in (0, 2)]
    edge_ref[...] = jnp.concatenate(pairs, axis=0).astype(B)
    rows = grad_ref.shape[0]
    grad = jnp.concatenate([grad_ref[0 : rows - EDGE, :], edge], axis=0)
    rows_ref[...] = jnp.dot(grad, test_ref[...], preferred_element_type=F)


def edge_and_rows(conv, act, after, taps, both, test):
    rows, width = conv.shape
    rank = test.shape[1]
    last = rows // EDGE - 1

    def whole(*shape):
        return pl.BlockSpec(shape, lambda i: (0, 0))

    return pl.pallas_call(
        edge_kernel,
        grid=(1,),
        out_shape=(
            jax.ShapeDtypeStruct((rows, rank), F),
            jax.ShapeDtypeStruct((EDGE, width // 4), B),
        ),
        in_specs=[
            pl.BlockSpec((EDGE, width), lambda i: (last, 0)),
            pl.BlockSpec((EDGE, width), lambda i: (last, 0)),
            whole(*after.shape),
            whole(*taps.shape),
            pl.BlockSpec((rows, width), lambda i: (1, 0)),
            whole(*test.shape),
        ],
        out_specs=(whole(rows, rank), whole(EDGE, width // 4)),
        scratch_shapes=[pltpu.VMEM((EDGE + 8, width), F)],
        compiler_params=pltpu.CompilerParams(vmem_limit_bytes=WIDE),
    )(conv, act, after, taps, both, test)


def middle_kernel(
    both_ref, rows_ref, edge_ref, weight_ref, sketch_ref, gram_ref, terms_ref,
    acts, grads, terms, right, weights, sketch, gram, in_sems, out_sems,
):
    shards, twice, width = both_ref.shape
    tokens = twice // 2
    groups, _, share, rank = rows_ref.shape
    chunks, each = grads.shape[:2]
    cols = width // chunks

    def acts_copy(i):
        return pltpu.make_async_copy(
            both_ref.at[:, 0:tokens, i * cols : (i + 1) * cols], acts.at[i], in_sems.at[i]
        )

    def grads_copy(i):
        return pltpu.make_async_copy(
            both_ref.at[i * each : (i + 1) * each, tokens:twice, :], grads.at[i], in_sems.at[chunks + i]
        )

    def terms_copy(i):
        return pltpu.make_async_copy(
            terms.at[i], terms_ref.at[i * each * tokens : (i + 1) * each * tokens, :], out_sems.at[i]
        )

    def rows_copy(g):
        return pltpu.make_async_copy(
            rows_ref.at[g], right.at[:, g * share : (g + 1) * share, :], in_sems.at[2 * chunks + 1 + g]
        )

    def sketch_copy(i):
        at = slice(i * cols, (i + 1) * cols)
        return pltpu.make_async_copy(sketch.at[at, :], sketch_ref.at[at, :], out_sems.at[chunks + i])

    weight_copy = pltpu.make_async_copy(weight_ref, weights, in_sems.at[2 * chunks])
    gram_copy = pltpu.make_async_copy(gram, gram_ref, out_sems.at[2 * chunks])
    for g in range(groups):
        rows_copy(g).start()
    for i in range(chunks):
        acts_copy(i).start()
    weight_copy.start()
    for i in range(chunks):
        grads_copy(i).start()
    for g in range(groups):
        rows_copy(g).wait()
    for i in range(chunks):
        acts_copy(i).wait()
        left = acts[i].reshape(shards * tokens, cols)
        part = dot(left, right[...].reshape(shards * tokens, rank), 0, 0, None)
        sketch[i * cols : (i + 1) * cols, :] = part
        sketch_copy(i).start()
        at = 0
        for r in range(rank // 128):
            block = dot(part[:, r * 128 : (r + 1) * 128], part[:, r * 128 :], 0, 0)
            for c in range(block.shape[1] // 128):
                piece = block[:, c * 128 : (c + 1) * 128]
                if i == 0:
                    gram[at : at + 128, :] = piece
                else:
                    gram[at : at + 128, :] += piece
                at += 128
    gram_copy.start()
    quarter = width // 4
    final = lax.broadcasted_iota(jnp.int32, (8, quarter), 0) >= 4
    weight_copy.wait()
    for i in range(chunks):
        grads_copy(i).wait()
        for z in range(each):
            edge = edge_ref[i * each + z].astype(F)
            old = grads[i, z, tokens - EDGE : tokens, :].astype(F)
            new = []
            for q in range(4):
                rows = edge[8 * (q // 2) : 8 * (q // 2) + 8, :]
                rows = rows if q % 2 else pltpu.roll(rows, 4, 0)
                new.append(jnp.where(final, rows, old[8:EDGE, q * quarter : (q + 1) * quarter]))
            new = jnp.concatenate([old[0:8, :], jnp.concatenate(new, axis=1)], axis=0)
            grads[i, z, tokens - EDGE : tokens, :] = new.astype(B)
        left = grads[i].reshape(each * tokens, width)
        terms[i] = dot(left, weights[...], 1, 1, None).astype(B)
        terms_copy(i).start()
    for i in range(chunks):
        sketch_copy(i).wait()
    gram_copy.wait()
    for i in range(chunks):
        terms_copy(i).wait()


def middle(gathered, rows, edges, weights):
    shards, twice, width = gathered.shape
    tokens = twice // 2
    rank = rows.shape[-1]
    blocks = rank // 128
    packed = blocks * (blocks + 1) // 2 * 128
    outs = weights.shape[0]
    chunks = 2
    each = shards // chunks
    return pl.pallas_call(
        middle_kernel,
        out_shape=(
            jax.ShapeDtypeStruct((width, rank), F),
            jax.ShapeDtypeStruct((packed, 128), F),
            jax.ShapeDtypeStruct((shards * tokens, outs), B),
        ),
        in_specs=[ANY, ANY, VMEM, ANY],
        out_specs=(ANY, ANY, ANY),
        scratch_shapes=[
            pltpu.VMEM((chunks, shards, tokens, width // chunks), B),
            pltpu.VMEM((chunks, each, tokens, width), B),
            pltpu.VMEM((chunks, each * tokens, outs), B),
            pltpu.VMEM((shards, tokens, rank), B),
            pltpu.VMEM(weights.shape, B),
            pltpu.VMEM((width, rank), F),
            pltpu.VMEM((packed, 128), F),
            pltpu.SemaphoreType.DMA((2 * chunks + 1 + rows.shape[0],)),
            pltpu.SemaphoreType.DMA((2 * chunks + 1,)),
        ],
        compiler_params=pltpu.CompilerParams(vmem_limit_bytes=MOST),
    )(gathered, rows, edges, weights)


def lane_of(x, l):
    return jnp.broadcast_to(x[:, l : l + 1], (8, 128))


def row_of(ref, r, c):
    return jnp.broadcast_to(ref[r : r + 1, c : c + 128], (8, 128))


def leaf(work, staged):
    sub = lax.broadcasted_iota(jnp.int32, (8, 128), 0)
    for p in range(16):
        top = 8 * p
        panel = work[top : top + 8, 0:128]
        left = [row_of(work, top + j, 0) for j in range(8)]
        right = [row_of(work, top + j, 128) for j in range(8)]
        e = {}
        for j in range(8):
            staged[8 * j : 8 * j + 8, :] = lane_of(panel, top + j)
            for i in range(j, 8):
                e[i, j] = row_of(staged, 8 * j + i, 0)
        inv = {}
        acc = {}
        for j in range(8):
            r = lax.rsqrt(e[j, j])
            low = {i: e[i, j] * r for i in range(j + 1, 8)}
            for i in range(j + 1, 8):
                for k in range(j + 1, i + 1):
                    e[i, k] = e[i, k] - low[i] * low[k]
            left[j] = left[j] * r
            right[j] = right[j] * r
            for k in range(j):
                inv[j, k] = -(acc[j, k] * r)
            inv[j, j] = r
            for i in range(j + 1, 8):
                left[i] = left[i] - low[i] * left[j]
                right[i] = right[i] - low[i] * right[j]
                for k in range(j + 1):
                    t = low[i] * inv[j, k]
                    acc[i, k] = acc[i, k] + t if (i, k) in acc else t
        rows = right[0]
        for j in range(1, 8):
            rows = jnp.where(sub == j, right[j], rows)
        work[top : top + 8, 128:256] = rows
        if p == 15:
            break
        whole_left = []
        whole_right = []
        for i in range(8):
            a = inv[i, i] * left[i]
            b = inv[i, i] * right[i]
            for j in range(i + 1, 8):
                a = a + inv[j, i] * left[j]
                b = b + inv[j, i] * right[j]
            whole_left.append(a)
            whole_right.append(b)
        for q in range(top + 8, 128, 8):
            old = work[q : q + 8, 0:128]
            by = [lane_of(old, top + j) for j in range(8)]
            work[q : q + 8, 0:128] = old - total_of(by[j] * whole_left[j] for j in range(8))
            work[q : q + 8, 128:256] -= total_of(by[j] * whole_right[j] for j in range(8))


def stage(k, blocks, m, work, staged):
    eye = (
        lax.broadcasted_iota(jnp.int32, (128, 128), 0)
        == lax.broadcasted_iota(jnp.int32, (128, 128), 1)
    ).astype(F)
    base = pl.multiple_of(k * 128, 128)
    work[:, 0:128] = m[pl.ds(base, 128), pl.ds(base, 128)]
    work[:, 128:256] = eye
    leaf(work, staged)
    width = blocks * 128

    def eliminate(top):
        end = top + 128
        inv = work[:, 128:256]
        if top > 0:
            m[top:end, 0:top] = dot(inv, m[top:end, 0:top], 1, 0)
        m[top:end, top:end] = inv
        if end < width:
            m[top:end, end:width] = dot(inv, m[top:end, end:width], 1, 0)
            change = dot(m[top:end, end:width], m[top:end, :], 0, 0)
            if top > 0:
                m[end:width, 0:top] -= change[:, 0:top]
            m[end:width, top:end] = -change[:, top:end]
            m[end:width, end:width] -= change[:, end:width]

    for which in range(blocks):
        pl.when(k == which)(functools.partial(eliminate, which * 128))


def factor_kernel(blocks, stages, gram_ref, m, work, staged):
    at = 0
    for r in range(blocks):
        for c in range(blocks):
            if c < r:
                m[r * 128 : (r + 1) * 128, c * 128 : (c + 1) * 128] = jnp.zeros((128, 128), F)
            else:
                m[r * 128 : (r + 1) * 128, c * 128 : (c + 1) * 128] = gram_ref[at : at + 128, :]
                at += 128

    def body(k, carry):
        stage(k, blocks, m, work, staged)
        return carry

    lax.fori_loop(0, stages, body, 0)


def apply_kernel(blocks, stages, scale, part_ref, sketch_ref, out_ref, m, work, staged):
    m[...] = part_ref[...]

    def body(k, carry):
        stage(k, blocks, m, work, staged)
        return carry

    lax.fori_loop(stages, blocks, body, 0)
    for r in range(blocks):
        for c in range(r + 1, blocks):
            m[r * 128 : (r + 1) * 128, c * 128 : (c + 1) * 128] = jnp.zeros((128, 128), F)
    rank = blocks * 128
    inv_hi, inv_lo = split(m[...] * scale)

    def rows(i, carry):
        at = pl.multiple_of(i * 512, 512)
        hi, lo = split(sketch_ref[pl.ds(at, 512), :])
        for c in range(0, rank, 256):
            end = min(c + 256, rank)
            left, right = inv_hi[c:end, 0:end], inv_lo[c:end, 0:end]
            out = dot(hi[:, 0:end], left, 1, 1, None)
            out += dot(hi[:, 0:end], right, 1, 1, None) + dot(lo[:, 0:end], left, 1, 1, None)
            out_ref[pl.ds(at, 512), c:end] = out.astype(B)
        return carry

    lax.fori_loop(0, sketch_ref.shape[0] // 512, rows, 0)


FIRST = 3


def factored(gram_packed, rank):
    blocks = rank // 128
    return pl.pallas_call(
        functools.partial(factor_kernel, blocks, FIRST),
        out_shape=jax.ShapeDtypeStruct((rank, rank), F),
        in_specs=[VMEM],
        out_specs=VMEM,
        scratch_shapes=[pltpu.VMEM((128, 256), F), pltpu.VMEM((64, 128), F)],
        compiler_params=pltpu.CompilerParams(vmem_limit_bytes=LIMIT),
    )(gram_packed)


def applied(part, sketch, scale):
    rank = sketch.shape[1]
    return pl.pallas_call(
        functools.partial(apply_kernel, rank // 128, FIRST, scale),
        out_shape=jax.ShapeDtypeStruct(sketch.shape, B),
        in_specs=[VMEM] * 2,
        out_specs=VMEM,
        scratch_shapes=[
            pltpu.VMEM((rank, rank), F),
            pltpu.VMEM((128, 256), F),
            pltpu.VMEM((64, 128), F),
        ],
        compiler_params=pltpu.CompilerParams(vmem_limit_bytes=LIMIT),
    )(part, sketch)


def local(layer_input, conv_out, act_grad, conv_kernel, in_proj, sketch_matrix):
    conv, act, taps = conv_out[0], act_grad[0], conv_kernel[0]
    shards = lax.axis_size("seq")
    groups = lax.axis_size("tensor")
    count = lax.axis_size("pipe")
    rank = sketch_matrix.shape[-1]
    after = lax.ppermute(
        jnp.concatenate([conv[:8], act[:8]], axis=0),
        "seq",
        [(i + 1, i) for i in range(shards - 1)],
    )
    both = front(conv, act, taps, layer_input[0])
    gathered = lax.all_gather(both, "seq", axis=0)
    row_terms, edge = edge_and_rows(conv, act, after, taps, both, sketch_matrix[0])
    row_terms = lax.all_to_all(row_terms.reshape(groups, -1, rank), "tensor", 0, 0, tiled=True)
    rows = jnp.sum(row_terms, axis=0).astype(B)
    small = lax.all_gather(jnp.concatenate([rows, edge], axis=1), "seq", axis=0)
    rows, edges = small[:, :, :rank], small[:, :, rank:]
    rows = lax.all_to_all(
        jnp.broadcast_to(rows[None], (groups,) + rows.shape), "tensor", 0, 0, tiled=True
    )
    gathered, rows, edges = lax.optimization_barrier((gathered, rows, edges))
    sketch, gram, terms = middle(gathered, rows, edges, in_proj[0])
    input_grad = lax.psum_scatter(terms, "tensor", scatter_dimension=0, tiled=True)
    gram = lax.all_to_all(gram.reshape(groups, -1, 128), "tensor", 0, 0, tiled=True)
    gram = lax.all_gather(jnp.sum(gram, axis=0), "tensor", axis=0, tiled=True)
    part = factored(gram, rank)
    input_grad, part = lax.optimization_barrier((input_grad, part))
    passed = lax.ppermute(input_grad, "pipe", [(i, (i - 1) % count) for i in range(count)])
    basis = applied(part, sketch, math.sqrt(D))
    return (passed[None], basis[None])


def solution(mesh):
    placed = (
        P("pipe", "seq", "tensor"),
        P("pipe", "seq", "tensor"),
        P("pipe", "seq", "tensor"),
        P("pipe", None, "tensor"),
        P("pipe", "seq", "tensor"),
        P("pipe", "tensor", None),
    )
    return jax.shard_map(
        local,
        mesh=mesh,
        in_specs=placed,
        out_specs=(P("pipe", "tensor", "seq"), P("pipe", "tensor", None)),
        check_vma=False,
    )
```
